128 devices in a mesh: var: 32 (over x, y, core), grp: 4 (over z).
Axes of the slice: x: 4, y: 4, z: 4, core: 2. Of those that a mesh axis runs over, the one named last changes fastest.
Arguments:
- series: bfloat16 [131072, 2048], P(('var', 'grp')), may hold values from -6 to 6
- w_embed: bfloat16 [2048, 512], replicated, may hold values from -0.125 to 0.125
- w_query: bfloat16 [512, 512], replicated, may hold values from -0.25 to 0.25
- w_key: bfloat16 [512, 512], replicated, may hold values from -0.25 to 0.25
- w_value: bfloat16 [512, 512], replicated, may hold values from -0.25 to 0.25
- w_out: bfloat16 [512, 512], replicated, may hold values from -0.25 to 0.25
- proj: bfloat16 [256, 131072], P(None, ('var', 'grp')), may hold values from -0.0625 to 0.0625
- cotangent: bfloat16 [131072, 512], P(('var', 'grp')), may hold values from -6 to 6
Outputs:
- output: bfloat16 [131072, 512], P(('var', 'grp'))
- grad_embed: float32 [2048, 512], replicated
- grad_attn: float32 [4, 512, 512], replicated
The draws below stay inside these ranges and needn't reach their ends.
All inputs are finite; a program needn't handle non-finite values.
Results may differ from the reference program's by a relative error of at most 0.019.
Values sent between devices are 32-bit elements; how exact they have to be, the bound alone decides.
A program may use at most 128 MiB of HBM per device.

```python
import math
import jax
import jax.numpy as jnp
from jax import lax

D = 512
HEADS = 8
LOOKBACK = 2048
KP = 256
V_DEV = 1024
VARIATES = 131072


def with_spikes(result, own_key, source, target, shards_of, factor):
    def block_of(dim):
        return (jnp.arange(result.shape[dim]) // (result.shape[dim] // shards_of)).reshape((-1,) + (1,) * (result.ndim - 1 - dim))

    one_side = jax.random.permutation(own_key, shards_of)[block_of(target)]
    far = (block_of(target) + shards_of // 2) % shards_of
    return jnp.where((block_of(source) == one_side) | (block_of(source) == far), factor * result, result)


def shard_levels(own_key, dims, shards, least, top_value):
    gain = 1.0
    for position, parts in shards:
        steps = jax.random.uniform(jax.random.fold_in(jax.random.fold_in(own_key, 6), position), (parts,), jnp.float32, least / len(shards), top_value / len(shards))
        gain = gain * jnp.repeat(jnp.exp(steps), dims[position] // parts).reshape((-1,) + (1,) * (len(dims) - 1 - position))
    return gain


def gaussian(key, extent, scale, most, shards=(), kind=jnp.bfloat16):
    entries = scale * jax.random.normal(key, extent, jnp.float32)
    if shards:
        entries = entries * shard_levels(key, extent, shards, -0.22, 0.18)
    return jnp.clip(entries, -most, most).astype(kind)


def gaussian_with(stream_key, shape, scale, bound, cuts, heavy, dtype=jnp.bfloat16):
    result = scale * jax.random.normal(stream_key, shape, jnp.float32)
    if cuts:
        result = result * shard_levels(stream_key, shape, cuts, -0.22, 0.18)
    return jnp.clip(with_spikes(result, jax.random.fold_in(stream_key, 3), *heavy), -bound, bound).astype(dtype)


def setup_inputs(seed: int = 0) -> dict:
    key_of = jax.random.split(jax.random.key(seed), 9)
    return {
        "series": gaussian(key_of[0], (VARIATES, LOOKBACK), 1.0, 6.0, ((0, 128),)),
        "w_embed": gaussian(key_of[1], (LOOKBACK, D), LOOKBACK ** -0.5, 0.125),
        "w_query": gaussian(key_of[2], (D, D), D ** -0.5, 0.25),
        "w_key": gaussian(key_of[3], (D, D), D ** -0.5, 0.25),
        "w_value": gaussian(key_of[4], (D, D), D ** -0.5, 0.25),
        "w_out": gaussian(key_of[5], (D, D), D ** -0.5, 0.25),
        "proj": gaussian_with(key_of[6], (KP, VARIATES), VARIATES ** -0.5, 0.0625, ((1, 128),), (1, 0, 128, 5.5)),
        "cotangent": gaussian(key_of[7], (VARIATES, D), 1.0, 6.0, ((0, 128),)),
    }


HIGH = lax.Precision.HIGHEST

def head_norm(values):
    shaped = values.reshape(values.shape[0], HEADS, -1)
    factor = lax.rsqrt(lax.optimization_barrier(jnp.mean(shaped * shaped, axis=-1, keepdims=True)) + 1e-06)
    return (shaped * factor, factor)

def norm_back(grad_n, normed, factor):
    return factor * (grad_n - normed * lax.optimization_barrier(jnp.mean(grad_n * normed, axis=-1, keepdims=True)))

def embed(series_rows, w_embed):
    return jnp.dot(series_rows, w_embed, preferred_element_type=jnp.float32).astype(jnp.bfloat16)

def reference(series, w_embed, w_query, w_key, w_value, w_out, proj, cotangent):
    blocks = VARIATES // V_DEV
    scale = 1.0 / math.sqrt(D // HEADS)
    series_b = series.reshape(blocks, V_DEV, LOOKBACK)
    proj_b = proj.reshape(KP, blocks, V_DEV).transpose(1, 0, 2)
    cot_b = cotangent.reshape(blocks, V_DEV, D)
    wk32 = w_key.astype(jnp.float32)
    wv32 = w_value.astype(jnp.float32)

    def project(carry, item):
        rows, pieces = item
        hid = embed(rows, w_embed)
        pf = pieces.astype(jnp.float32)
        keys = jnp.dot(hid, w_key, preferred_element_type=jnp.float32)
        values = jnp.dot(hid, w_value, preferred_element_type=jnp.float32)
        return ((carry[0] + jnp.dot(pf, keys, precision=HIGH), carry[1] + jnp.dot(pf, values, precision=HIGH)), None)
    zero = jnp.zeros((KP, D), jnp.float32)
    (keyproj, valproj), _ = lax.scan(project, (zero, zero), (series_b, proj_b))
    val_b = valproj.astype(jnp.bfloat16)
    key_n, key_r = head_norm(keyproj)
    key_nb = key_n.astype(jnp.bfloat16)
    val_h = val_b.reshape(KP, HEADS, -1)
    val_f = valproj.reshape(KP, HEADS, -1)

    def attend(carry, item):
        rows, cot = item
        hid = embed(rows, w_embed)
        query = jnp.dot(hid, w_query, preferred_element_type=jnp.float32)
        query_n, query_r = head_norm(query)
        query_nb = query_n.astype(jnp.bfloat16)
        scores = jnp.einsum('nhd,khd->nhk', query_nb.astype(jnp.float32), key_nb.astype(jnp.float32)) * scale
        expo = jnp.exp(scores)
        probs = expo / lax.optimization_barrier(jnp.sum(expo, axis=-1, keepdims=True))
        probs_b = probs.astype(jnp.bfloat16)
        attended = jnp.einsum('nhk,khd->nhd', probs_b.astype(jnp.float32), val_h.astype(jnp.float32))
        attended = attended.astype(jnp.bfloat16).reshape(V_DEV, D)
        output = (hid.astype(jnp.float32) + jnp.dot(attended, w_out, preferred_element_type=jnp.float32)).astype(jnp.bfloat16)
        grad_att = jnp.dot(cot, w_out.T, preferred_element_type=jnp.float32).astype(jnp.bfloat16).reshape(V_DEV, HEADS, -1)
        gw_out = jnp.dot(attended.T, cot, preferred_element_type=jnp.float32)
        grad_att32 = grad_att.astype(jnp.float32)
        grad_probs = jnp.einsum('nhd,khd->nhk', grad_att32, val_f, precision=HIGH)
        grad_val = jnp.einsum('nhk,nhd->khd', probs_b.astype(jnp.float32), grad_att32).reshape(KP, D)
        grad_scores = (probs * (grad_probs - lax.optimization_barrier(jnp.sum(probs * grad_probs, axis=-1, keepdims=True))) * scale).astype(jnp.bfloat16)
        gs32 = grad_scores.astype(jnp.float32)
        grad_qn = jnp.einsum('nhk,khd->nhd', gs32, key_nb.astype(jnp.float32))
        grad_kn = jnp.einsum('nhk,nhd->khd', gs32, query_nb.astype(jnp.float32)).reshape(KP, D)
        grad_query = norm_back(grad_qn, query_n, query_r).reshape(V_DEV, D).astype(jnp.bfloat16)
        gw_query = jnp.dot(hid.T, grad_query, preferred_element_type=jnp.float32)
        new = (carry[0] + grad_kn, carry[1] + grad_val, carry[2] + gw_query, carry[3] + gw_out)
        return (new, (output, grad_query))
    zero_w = jnp.zeros((D, D), jnp.float32)
    (grad_kn, grad_val, gw_query, gw_out), (outputs, grad_queries) = lax.scan(attend, (zero, zero, zero_w, zero_w), (series_b, cot_b))
    grad_key = norm_back(grad_kn.reshape(KP, HEADS, -1), key_n, key_r).reshape(KP, D)

    def finish(carry, item):
        rows, pieces, cot, grad_query = item
        hid = embed(rows, w_embed)
        pf = pieces.astype(jnp.float32)
        grad_k = jnp.dot(pf.T, grad_key, precision=HIGH)
        grad_v = jnp.dot(pf.T, grad_val, precision=HIGH)
        hid32 = hid.astype(jnp.float32)
        gw_key = jnp.dot(hid32.T, grad_k, precision=HIGH)
        gw_value = jnp.dot(hid32.T, grad_v, precision=HIGH)
        from_kv = jnp.dot(grad_k, wk32.T, precision=HIGH) + jnp.dot(grad_v, wv32.T, precision=HIGH)
        grad_hid = (cot.astype(jnp.float32) + jnp.dot(grad_query, w_query.T, preferred_element_type=jnp.float32) + from_kv).astype(jnp.bfloat16)
        gw_embed = jnp.dot(rows.T, grad_hid, preferred_element_type=jnp.float32)
        return ((carry[0] + gw_embed, carry[1] + gw_key, carry[2] + gw_value), None)
    zero_e = jnp.zeros((LOOKBACK, D), jnp.float32)
    (gw_embed, gw_key, gw_value), _ = lax.scan(finish, (zero_e, zero_w, zero_w), (series_b, proj_b, cot_b, grad_queries))
    norm = 1.0 / math.sqrt(VARIATES)
    grad_attn = jnp.stack([gw_query, gw_key, gw_value, gw_out]) * norm
    return (outputs.reshape(VARIATES, D), gw_embed * norm, grad_attn)
```

```python
import functools
import math

import jax
import jax.numpy as jnp
from jax import lax
from jax.experimental import pallas as pl
from jax.experimental.pallas import tpu as pltpu
from jax.sharding import PartitionSpec as P

HEADS = 8
MESH = pl.DeviceIdType.MESH
F32 = jnp.float32
BF16 = jnp.bfloat16
VMEM = pltpu.VMEM


def head_norm(values):
    shaped = values.reshape(values.shape[0], HEADS, -1)
    factor = lax.rsqrt(jnp.mean(shaped * shaped, axis=-1, keepdims=True) + 1e-06)
    return (shaped * factor, factor)


def norm_back(grad_n, normed, factor):
    return factor * (grad_n - normed * jnp.mean(grad_n * normed, axis=-1, keepdims=True))


def contract_rows(left, right, precision=None):
    return lax.dot_general(
        left,
        right,
        (((0,), (0,)), ((), ())),
        preferred_element_type=F32,
        precision=precision,
    )


def split_parts(values, axis):
    upper = values.astype(BF16)
    rest = values - upper.astype(F32)
    middle = rest.astype(BF16)
    lower = (rest - middle.astype(F32)).astype(BF16)
    return jnp.concatenate([upper, middle, lower], axis)


def fold_parts(values, axis):
    first, second, third = jnp.split(values, 3, axis)
    return first + second + third


def position():
    var = lax.axis_index("var")
    return {
        "x": lax.div(var, 8),
        "y": lax.rem(lax.div(var, 2), 4),
        "c": lax.rem(var, 2),
        "z": lax.axis_index("grp"),
    }


def moved(place, **steps):
    there = dict(place)
    for axis, step in steps.items():
        there[axis] = lax.rem(place[axis] + step, 2 if axis == "c" else 4)
    return (there["x"] * 8 + there["y"] * 2 + there["c"], there["z"])


def greet(devices):
    barrier = pltpu.get_barrier_semaphore()
    for device in devices:
        pl.semaphore_signal(barrier, inc=1, device_id=device, device_id_type=MESH)
    return lambda: pl.semaphore_wait(barrier, len(devices))


def sum_small_kernel(in_ref, out_ref, half, from_core, from_plane, from_x, send, recv):
    here = position()
    core, plane = here["c"], here["y"] * 4 + here["z"]
    base = core * 512

    def plane_device(step):
        there = lax.rem(plane + step, 16)
        return (here["x"] * 8 + lax.div(there, 4) * 2 + core, lax.rem(there, 4))

    others = [moved(here, c=1)]
    others += [moved(here, x=step) for step in (1, 2, 3)]
    others += [plane_device(step) for step in range(1, 16)]
    greet(others)()
    count = [0]

    def copy(src, dst, device):
        slot = count[0]
        count[0] += 1
        made = pltpu.make_async_remote_copy(
            src_ref=src,
            dst_ref=dst,
            send_sem=send.at[slot],
            recv_sem=recv.at[slot],
            device_id=device,
            device_id_type=MESH,
        )
        made.start()
        return made

    across = copy(in_ref.at[pl.ds((1 - core) * 512, 512)], from_core, moved(here, c=1))
    across.wait()
    half[...] = in_ref[pl.ds(pl.multiple_of(base, 512), 512)] + from_core[...]
    sent = []
    for step in range(1, 16):
        there = lax.rem(plane + step, 16)
        sent.append(
            copy(half.at[pl.ds(there * 32, 32)], from_plane.at[step], plane_device(step))
        )
    own = pl.multiple_of(plane * 32, 32)
    total = half[pl.ds(own, 32)]
    for made in sent:
        made.wait_recv()
    for step in range(1, 16):
        total = total + from_plane[step]
    from_x[here["x"]] = total
    shares = [
        copy(from_x.at[here["x"]], from_x.at[here["x"]], moved(here, x=step))
        for step in (1, 2, 3)
    ]
    for made in shares:
        made.wait_recv()
    whole = (from_x[0] + from_x[1]) + (from_x[2] + from_x[3])
    mine = out_ref.at[pl.ds(base + own, 32)]
    mine[...] = whole
    spread = [copy(mine, mine, plane_device(step)) for step in range(1, 16)]
    passed = [copy(mine, mine, moved(here, c=1))]
    for step in range(1, 16):
        spread[step - 1].wait_recv()
        origin = lax.rem(plane + 16 - step, 16)
        piece = out_ref.at[pl.ds(base + origin * 32, 32)]
        passed.append(copy(piece, piece, moved(here, c=1)))
    for made in passed:
        made.wait_recv()
    for made in sent + shares + spread + passed:
        made.wait_send()


def sum_small(values):
    copies = 1 + 15 + 3 + 15 + 16
    return pl.pallas_call(
        sum_small_kernel,
        out_shape=jax.ShapeDtypeStruct((1024, 128), F32),
        in_specs=[pl.BlockSpec(memory_space=VMEM)],
        out_specs=pl.BlockSpec(memory_space=VMEM),
        scratch_shapes=[
            VMEM((512, 128), F32),
            VMEM((512, 128), F32),
            VMEM((16, 32, 128), F32),
            VMEM((4, 32, 128), F32),
            pltpu.SemaphoreType.DMA((copies,)),
            pltpu.SemaphoreType.DMA((copies,)),
        ],
        compiler_params=pltpu.CompilerParams(collective_id=0, has_side_effects=True),
    )(values)


ORDERS = (("x", "y", "z"), ("y", "z", "x"), ("z", "x", "y"))
UNITS = 6


def sum_large_kernel(in_ref, out_ref, work, from_core, ring1, ring2, last, send, recv):
    here = position()
    core = here["c"]
    base = core * 512
    ready = greet(
        [moved(here, c=1)]
        + [moved(here, **{axis: step}) for axis in "xyz" for step in (1, 2, 3)]
    )
    ready()
    count = [0]
    sent = []

    def copy(src, dst, device):
        slot = count[0]
        count[0] += 1
        made = pltpu.make_async_remote_copy(
            src_ref=src,
            dst_ref=dst,
            send_sem=send.at[slot],
            recv_sem=recv.at[slot],
            device_id=device,
            device_id_type=MESH,
        )
        made.start()
        sent.append(made)
        return made

    groups = range(3)
    units = [pl.ds(group * UNITS, UNITS) for group in groups]

    def rows(start, size, step):
        return pl.ds(pl.multiple_of(start, step), size)

    across = [
        copy(
            in_ref.at[units[group], rows((1 - core) * 512, 512, 512)],
            from_core.at[group],
            moved(here, c=1),
        )
        for group in groups
    ]
    for group in groups:
        across[group].wait_recv()

        @pl.loop(0, UNITS)
        def _(unit):
            work[group, unit] = (
                in_ref[group * UNITS + unit, rows(base, 512, 512)] + from_core[group, unit]
            )

    offset = [0, 0, 0]
    for level, size, ring in ((0, 128, ring1), (1, 32, ring2)):
        half = size // 2

        def part(group, step, which):
            axis = ORDERS[group][level]
            chunk = lax.rem(here[axis] + step, 4)
            return (group, slice(None), rows(offset[group] + chunk * size + which * half, half, half))

        state = []
        for group in groups:
            axis = ORDERS[group][level]
            up, down = moved(here, **{axis: 1}), moved(here, **{axis: 3})
            state.append(
                (
                    copy(work.at[part(group, 2, 0)], ring.at[group, 0], up),
                    copy(work.at[part(group, 2, 1)], ring.at[group, 1], down),
                    copy(work.at[part(group, 1, 1)], ring.at[group, 2], up),
                    copy(work.at[part(group, 3, 0)], ring.at[group, 3], down),
                    up,
                    down,
                )
            )
        more = []
        for group in groups:
            relay_a, relay_b, _, _, up, down = state[group]
            relay_a.wait_recv()
            where = part(group, 1, 0)
            work[where] = work[where] + ring[group, 0]
            more_a = copy(work.at[where], ring.at[group, 4], up)
            relay_b.wait_recv()
            where = part(group, 3, 1)
            work[where] = work[where] + ring[group, 1]
            more.append((more_a, copy(work.at[where], ring.at[group, 5], down)))
        for group in groups:
            _, _, direct_b, direct_a, _, _ = state[group]
            more_a, more_b = more[group]
            direct_a.wait_recv()
            more_a.wait_recv()
            where = part(group, 0, 0)
            work[where] = work[where] + ring[group, 3] + ring[group, 4]
            direct_b.wait_recv()
            more_b.wait_recv()
            where = part(group, 0, 1)
            work[where] = work[where] + ring[group, 2] + ring[group, 5]
        for group in groups:
            offset[group] = offset[group] + here[ORDERS[group][level]] * size

    direct = []
    for group in groups:
        axis = ORDERS[group][2]
        direct.append(
            [
                copy(
                    work.at[
                        group,
                        :,
                        rows(offset[group] + lax.rem(here[axis] + step, 4) * 8, 8, 8),
                    ],
                    last.at[group, step - 1],
                    moved(here, **{axis: step}),
                )
                for step in (1, 2, 3)
            ]
        )
    spread = []
    for group in groups:
        axis = ORDERS[group][2]
        for made in direct[group]:
            made.wait_recv()
        own = offset[group] + here[axis] * 8
        mine = (units[group], rows(base + own, 8, 8))
        out_ref[mine] = (
            work[group, :, rows(own, 8, 8)] + last[group, 0] + last[group, 1] + last[group, 2]
        )
        spread.append(
            [
                copy(out_ref.at[mine], out_ref.at[mine], moved(here, **{axis: step}))
                for step in (1, 2, 3)
            ]
        )
    for group in groups:
        for made in spread[group]:
            made.wait_recv()

    arrivals = []
    for level, size in ((1, 32), (0, 128)):
        half = size // 2
        state = []

        def piece(group, step, start=0, length=None):
            axis = ORDERS[group][level]
            chunk = lax.rem(here[axis] + step, 4)
            length = size if length is None else length
            return out_ref.at[
                units[group], rows(base + offset[group] + chunk * size + start, length, half)
            ]

        for group in groups:
            axis = ORDERS[group][level]
            offset[group] = offset[group] - here[axis] * size
            up, down = moved(here, **{axis: 1}), moved(here, **{axis: 3})
            own = piece(group, 0)
            state.append((copy(own, own, up), copy(own, own, down), up, down))
            if level == 0:
                arrivals.append(copy(own, own, moved(here, c=1)))
        forwards = []
        for group in groups:
            from_down, from_up, up, down = state[group]
            from_down.wait_recv()
            got = piece(group, 3, 0, half)
            forward_a = copy(got, got, up)
            from_up.wait_recv()
            got = piece(group, 1, half, half)
            forwards.append((forward_a, copy(got, got, down)))
            if level == 0:
                for step in (1, 3):
                    got = piece(group, step)
                    arrivals.append(copy(got, got, moved(here, c=1)))
        for group in groups:
            for made in forwards[group]:
                made.wait_recv()
            if level == 0:
                got = piece(group, 2)
                arrivals.append(copy(got, got, moved(here, c=1)))
    for made in arrivals:
        made.wait_recv()
    for made in sent:
        made.wait_send()


def sum_large(values):
    copies = 3 * (1 + 6 + 6 + 3 + 3 + 4 + 4 + 4)
    return pl.pallas_call(
        sum_large_kernel,
        out_shape=jax.ShapeDtypeStruct((18, 1024, 128), F32),
        in_specs=[pl.BlockSpec(memory_space=VMEM)],
        out_specs=pl.BlockSpec(memory_space=VMEM),
        scratch_shapes=[
            VMEM((3, UNITS, 512, 128), F32),
            VMEM((3, UNITS, 512, 128), F32),
            VMEM((3, 6, UNITS, 64, 128), F32),
            VMEM((3, 6, UNITS, 16, 128), F32),
            VMEM((3, 3, UNITS, 8, 128), F32),
            pltpu.SemaphoreType.DMA((copies,)),
            pltpu.SemaphoreType.DMA((copies,)),
        ],
        compiler_params=pltpu.CompilerParams(
            collective_id=1, has_side_effects=True, vmem_limit_bytes=56 * 1024 * 1024
        ),
    )(values)


def to_units(values):
    rows, columns = values.shape
    lanes = values.reshape(rows, columns // 128, 128).transpose(1, 0, 2)
    return lanes.reshape(-1, 1024, 128)


def from_units(units, rows, columns):
    lanes = units.reshape(columns // 128, rows, 128)
    return lanes.transpose(1, 0, 2).reshape(rows, columns)


def local(series, w_embed, w_query, w_key, w_value, w_out, proj, cotangent):
    rows = series.shape[0]
    proj_rows = proj.shape[0]
    width = w_query.shape[0]
    scale = 1.0 / math.sqrt(width // HEADS)
    total_rows = rows * lax.axis_size("var") * lax.axis_size("grp")
    hid = jnp.dot(series, w_embed, preferred_element_type=F32).astype(BF16)
    kv_weights = jnp.concatenate([w_key, w_value], 1)
    kv_back = jnp.concatenate([w_key.T, w_value.T], 0)
    ph_part = jnp.dot(proj, hid, preferred_element_type=F32)
    ph = from_units(sum_small(to_units(ph_part)[0])[None], proj_rows, width)
    kv = fold_parts(jnp.dot(split_parts(ph, 0), kv_weights, preferred_element_type=F32), 0)
    keyproj, valproj = kv[:, :width], kv[:, width:]
    key_n, key_r = head_norm(keyproj)
    key_nb = key_n.astype(BF16)
    val_parts = split_parts(valproj, 0).reshape(3 * proj_rows, HEADS, -1)
    val_h = val_parts[:proj_rows]
    query = jnp.dot(hid, w_query, preferred_element_type=F32)
    query_n, query_r = head_norm(query)
    query_nb = query_n.astype(BF16)
    scores = (
        jnp.einsum("nhd,khd->nhk", query_nb, key_nb, preferred_element_type=F32) * scale
    )
    expo = jnp.exp(scores)
    probs = expo / jnp.sum(expo, axis=-1, keepdims=True)
    probs_b = probs.astype(BF16)
    attended = jnp.einsum("nhk,khd->nhd", probs_b, val_h, preferred_element_type=F32)
    attended = attended.astype(BF16).reshape(rows, width)
    output = (
        hid.astype(F32) + jnp.dot(attended, w_out, preferred_element_type=F32)
    ).astype(BF16)
    grad_att = (
        jnp.dot(cotangent, w_out.T, preferred_element_type=F32)
        .astype(BF16)
        .reshape(rows, HEADS, -1)
    )
    gw_out = contract_rows(attended, cotangent)
    grad_probs = fold_parts(
        jnp.einsum("nhd,khd->nhk", grad_att, val_parts, preferred_element_type=F32), 2
    )
    grad_val = jnp.einsum(
        "nhk,nhd->khd", probs_b, grad_att, preferred_element_type=F32
    ).reshape(proj_rows, width)
    grad_scores = (
        probs * (grad_probs - jnp.sum(probs * grad_probs, axis=-1, keepdims=True)) * scale
    ).astype(BF16)
    grad_qn = jnp.einsum("nhk,khd->nhd", grad_scores, key_nb, preferred_element_type=F32)
    grad_kn = jnp.einsum(
        "nhk,nhd->khd", grad_scores, query_nb, preferred_element_type=F32
    ).reshape(proj_rows, width)
    grad_query = norm_back(grad_qn, query_n, query_r).reshape(rows, width).astype(BF16)
    gw_query = contract_rows(hid, grad_query)
    grad_hid = (
        cotangent.astype(F32) + jnp.dot(grad_query, w_query.T, preferred_element_type=F32)
    ).astype(BF16)
    gw_embed = contract_rows(series, grad_hid)
    proj_series = jnp.dot(proj, series, preferred_element_type=F32)
    totals = sum_large(
        jnp.concatenate(
            [
                to_units(part)
                for part in (gw_embed, proj_series, gw_query, gw_out, grad_kn, grad_val)
            ],
            0,
        )
    )
    gw_embed = from_units(totals[0:8], 2048, width)
    proj_series = from_units(totals[8:12], proj_rows, 2048)
    gw_query = from_units(totals[12:14], width, width)
    gw_out = from_units(totals[14:16], width, width)
    grad_kn = from_units(totals[16:17], proj_rows, width)
    grad_val = from_units(totals[17:18], proj_rows, width)
    grad_key = norm_back(grad_kn.reshape(proj_rows, HEADS, -1), key_n, key_r).reshape(
        proj_rows, width
    )
    grad_both = jnp.concatenate([grad_key, grad_val], 1)
    back = fold_parts(
        jnp.dot(split_parts(grad_both, 0), kv_back, preferred_element_type=F32), 0
    )
    high = lax.Precision.HIGHEST
    gw_embed = gw_embed + contract_rows(proj_series, back, high)
    gw_key = contract_rows(ph, grad_key, high)
    gw_value = contract_rows(ph, grad_val, high)
    norm = 1.0 / math.sqrt(total_rows)
    grad_attn = jnp.stack([gw_query, gw_key, gw_value, gw_out]) * norm
    return (output, gw_embed * norm, grad_attn)


def solution(mesh):
    return jax.shard_map(
        local,
        mesh=mesh,
        in_specs=(
            P(("var", "grp"), None),
            P(),
            P(),
            P(),
            P(),
            P(),
            P(None, ("var", "grp")),
            P(("var", "grp"), None),
        ),
        out_specs=(P(("var", "grp"), None), P(), P()),
        check_vma=False,
    )
```

```python
import functools
import math

import jax
import jax.numpy as jnp
from jax import lax
from jax.experimental import pallas as pl
from jax.experimental.pallas import tpu as pltpu
from jax.sharding import PartitionSpec as P

MESH = pl.DeviceIdType.MESH
F32 = jnp.float32
BF16 = jnp.bfloat16
VMEM = pltpu.VMEM
ROWS = 1024
WIDTH = 512
LOOKBACK = 2048
KP = 256
PAIRS = 4
BLOCK = 256
BLOCKS = ROWS // BLOCK
NORM = 1.0 / math.sqrt(131072.0)
LAST_STAGE = 99


def dot(left, right, dims=((1,), (0,))):
    return lax.dot_general(left, right, (dims, ((), ())), preferred_element_type=F32)


def dot_t(left, right):
    return dot(left, right, ((1,), (1,)))


def hi_lo(values):
    upper = values.astype(BF16)
    return upper, (values - upper.astype(F32)).astype(BF16)


def rows(start, size, step=None):
    return pl.ds(pl.multiple_of(start, step or size), size)


def position():
    var = lax.axis_index("var")
    return {
        "x": lax.div(var, 8),
        "y": lax.rem(lax.div(var, 2), 4),
        "c": lax.rem(var, 2),
        "z": lax.axis_index("grp"),
    }


def moved(place, **steps):
    there = dict(place)
    for axis, step in steps.items():
        there[axis] = lax.rem(place[axis] + step, 2 if axis == "c" else 4)
    return (there["x"] * 8 + there["y"] * 2 + there["c"], there["z"])


class Copies:
    def __init__(self, send, recv):
        self.send, self.recv = send, recv
        self.count = 0
        self.waiting = []

    def __call__(self, src, dst, device):
        slot = self.count
        self.count += 1
        made = pltpu.make_async_remote_copy(
            src_ref=src,
            dst_ref=dst,
            send_sem=self.send.at[slot],
            recv_sem=self.recv.at[slot],
            device_id=device,
            device_id_type=MESH,
        )
        made.start()
        self.waiting.append(made)
        return made

    def drain(self):
        for made in self.waiting:
            made.wait_send()
        self.waiting = []


X, Y, Z = ("x", "y", "z"), ("y", "z", "x"), ("z", "x", "y")


class Sum:
    def __init__(self, here, copies, groups, bufs):
        self.here, self.copy, self.groups = here, copies, groups
        self.data, self.half, self.one, self.two, self.three, self.out = bufs
        self.base = here["c"] * 512
        self.across = []
        self.made = {}

    def core(self, group):
        _, start, size = self.groups[group]
        units = pl.ds(start, size)
        self.across.append(
            self.copy(
                self.data.at[units, rows((1 - self.here["c"]) * 512, 512)],
                self.half.at[units],
                moved(self.here, c=1),
            )
        )

    def place(self, group, level):
        order = self.groups[group][0]
        sizes = (128, 32, 8)
        at = self.base
        for axis, size in zip(order[:level], sizes[:level]):
            at = at + self.here[axis] * size
        return at

    def scatter(self, level, group):
        order, start, size = self.groups[group]
        axis = order[level]
        extent = (128, 32, 8)[level]
        buffer = (self.one, self.two, self.three)[level]
        at = self.place(group, level)
        self.made[group] = [
            self.copy(
                self.data.at[
                    pl.ds(start, size),
                    rows(at + lax.rem(self.here[axis] + step, 4) * extent, extent),
                ],
                buffer.at[step - 1, pl.ds(start, size)],
                moved(self.here, **{axis: step}),
            )
            for step in (2, 1, 3)
        ]

    def gather(self, level, group):
        order, start, size = self.groups[group]
        axis = order[level]
        extent = (128, 32, 8)[level]
        own = self.out.at[pl.ds(start, size), rows(self.place(group, level + 1), extent)]
        self.made[group] = [
            self.copy(own, own, moved(self.here, **{axis: step})) for step in (2, 1, 3)
        ]
        return own

    def step1(self):
        for group, (_, start, size) in enumerate(self.groups):
            self.across[group].wait_recv()

            @pl.loop(start, start + size)
            def _(unit):
                where = (unit, rows(self.base, 512))
                self.data[where] = self.data[where] + self.half[unit]

            self.scatter(0, group)

    def reduced(self, level, group):
        _, start, size = self.groups[group]
        extent = (128, 32, 8)[level]
        buffer = (self.one, self.two, self.three)[level]
        for made in self.made[group]:
            made.wait_recv()
        units = pl.ds(start, size)
        where = (units, rows(self.place(group, level + 1), extent))
        total = (self.data[where] + buffer[0, units]) + (buffer[1, units] + buffer[2, units])
        if level == 2:
            self.out[where] = total
        else:
            self.data[where] = total

    def step2(self):
        for group in range(len(self.groups)):
            self.reduced(0, group)
            self.scatter(1, group)

    def step3(self):
        for group in range(len(self.groups)):
            self.reduced(1, group)
            self.scatter(2, group)

    def step4(self):
        for group in range(len(self.groups)):
            self.reduced(2, group)
            self.gather(2, group)

    def gathered(self, group):
        for made in self.made[group]:
            made.wait_recv()

    def step5(self):
        for group in range(len(self.groups)):
            self.gathered(group)
            self.gather(1, group)

    def step6(self):
        self.passed = []
        for group in range(len(self.groups)):
            self.gathered(group)
            own = self.gather(0, group)
            self.passed.append([self.copy(own, own, moved(self.here, c=1))])

    def step7(self):
        for group, (order, start, size) in enumerate(self.groups):
            for made, step in zip(self.made[group], (2, 1, 3)):
                made.wait_recv()
                chunk = lax.rem(self.here[order[0]] + 4 - step, 4)
                piece = self.out.at[pl.ds(start, size), rows(self.base + chunk * 128, 128)]
                self.passed[group].append(self.copy(piece, piece, moved(self.here, c=1)))

    def step8(self, group):
        for made in self.passed[group]:
            made.wait_recv()

    def all8(self):
        for group in range(len(self.groups)):
            self.step8(group)


def sum_bufs(units):
    return [
        VMEM((units, 1024, 128), F32),
        VMEM((units, 512, 128), F32),
        VMEM((3, units, 128, 128), F32),
        VMEM((3, units, 32, 128), F32),
        VMEM((3, units, 8, 128), F32),
        VMEM((units, 1024, 128), F32),
    ]


S_GROUPS = ((X, 0, 1), (Y, 1, 2), (Z, 3, 1))
Q_GROUPS = ((X, 0, 1), (Y, 1, 1), (Z, 2, 1))
E_GROUPS = (((X, 0, 2), (Y, 2, 1), (Z, 3, 1)), ((Z, 0, 2), (Y, 2, 1), (X, 3, 1)))

SHAPES = dict(
    series=((ROWS, LOOKBACK), BF16),
    w_embed=((LOOKBACK, WIDTH), BF16),
    w_query=((WIDTH, WIDTH), BF16),
    w_key=((WIDTH, WIDTH), BF16),
    w_value=((WIDTH, WIDTH), BF16),
    w_out=((WIDTH, WIDTH), BF16),
    proj=((KP, ROWS), BF16),
    cot=((ROWS, WIDTH), BF16),
    series_t=((LOOKBACK, ROWS), BF16),
    hid=((ROWS, WIDTH), BF16),
    hid_t=((WIDTH, ROWS), BF16),
    q_r=((PAIRS, ROWS, 128), F32),
    q_n=((PAIRS, ROWS, 128), BF16),
    g_att=((PAIRS, ROWS, 128), BF16),
    att=((PAIRS, ROWS, 128), BF16),
    g_query=((PAIRS, ROWS, 128), BF16),
    g_hid=((ROWS, WIDTH), BF16),
    key_n=((PAIRS, KP, 128), F32),
    key_r=((PAIRS, KP, 128), F32),
    key_in=((PAIRS, 128, 512), BF16),
    key_out=((PAIRS, 512, 128), BF16),
    val_in=((PAIRS, 256, 512), BF16),
    val_out=((PAIRS, 512, 128), BF16),
    ph_in=((1024, 128), F32),
    ph_half=((512, 128), F32),
    ph_core=((512, 128), F32),
    ph_plane=((16, 32, 128), F32),
    ph_x=((4, 32, 128), F32),
    ph=((1024, 128), F32),
    ph_t=((2, WIDTH, KP), BF16),
    gk=((2, KP, WIDTH), BF16),
    gv=((2, KP, WIDTH), BF16),
    back=((2, KP, WIDTH), BF16),
    out=((ROWS, WIDTH), BF16),
)
LOADS = ("w_embed", "proj", "cot", "w_out", "w_query", "w_key", "w_value")
N_COPIES = 50 + 5 * 3 * 23


def layer_kernel(*refs):
    names = ("series", "w_embed", "w_query", "w_key", "w_value", "w_out", "proj", "cot")
    hbm = dict(zip(names, refs[:8]))
    out_hbm, embed_hbm, attn_hbm = refs[8:11]
    refs = refs[11:]
    v = dict(zip(SHAPES, refs[: len(SHAPES)]))
    refs = refs[len(SHAPES) :]
    s_bufs, q0_bufs, q1_bufs, e0_bufs, e1_bufs = (refs[6 * i : 6 * i + 6] for i in range(5))
    send, recv, load_sem, store_sem = refs[30:]
    here = position()
    core, plane = here["c"], here["y"] * 4 + here["z"]
    base = core * 512

    def plane_device(step):
        there = lax.rem(plane + step, 16)
        return (here["x"] * 8 + lax.div(there, 4) * 2 + core, lax.rem(there, 4))

    loads = {}
    for slot, name in enumerate(LOADS):
        loads[name] = pltpu.make_async_copy(hbm[name], v[name], load_sem.at[slot])
    series_loads = []
    for block in range(BLOCKS):
        where = pl.ds(block * BLOCK, BLOCK)
        series_loads.append(
            pltpu.make_async_copy(
                hbm["series"].at[where], v["series"].at[where], load_sem.at[len(LOADS) + block]
            )
        )
    loads["w_embed"].start()
    for made in series_loads:
        made.start()
    for name in LOADS[1:]:
        loads[name].start()

    barrier = pltpu.get_barrier_semaphore()
    others = [moved(here, c=1)]
    others += [moved(here, x=step) for step in (1, 2, 3)]
    others += [plane_device(step) for step in range(1, 16)]
    for device in others:
        pl.semaphore_signal(barrier, inc=1, device_id=device, device_id_type=MESH)

    copies = Copies(send, recv)
    sum_s = Sum(here, copies, S_GROUPS, s_bufs)
    sum_q = [Sum(here, copies, Q_GROUPS, bufs) for bufs in (q0_bufs, q1_bufs)]
    sum_e = [Sum(here, copies, E_GROUPS[i], bufs) for i, bufs in enumerate((e0_bufs, e1_bufs))]

    lane = lax.broadcasted_iota(jnp.int32, (256, 128), 1) & 64
    row = lax.broadcasted_iota(jnp.int32, (256, 128), 0) & 64
    ones = jnp.where(lane == row, 1.0 / 64, 0.0).astype(BF16)

    def head_mean(values):
        return dot(jnp.concatenate(hi_lo(values), 1), ones)

    loads["w_embed"].wait()
    for block in range(BLOCKS):
        series_loads[block].wait()
        where = pl.ds(block * BLOCK, BLOCK)
        v["hid"][where] = dot(v["series"][where], v["w_embed"][...]).astype(BF16)
    loads["proj"].wait()
    part = dot(v["proj"][...], v["hid"][...])
    for pair in range(PAIRS):
        v["ph_in"][pl.ds(pair * 256, 256)] = part[:, pair * 128 : pair * 128 + 128]

    pl.semaphore_wait(barrier, len(others))
    across = copies(v["ph_in"].at[rows((1 - core) * 512, 512)], v["ph_core"], moved(here, c=1))

    loads["cot"].wait()
    loads["w_out"].wait()

    @pl.loop(0, BLOCKS)
    def _(block):
        where = rows(block * BLOCK, BLOCK)
        grad = dot_t(v["cot"][where], v["w_out"][...]).astype(BF16)
        for pair in range(PAIRS):
            v["g_att"][pair, where] = grad[:, pair * 128 : pair * 128 + 128]

    across.wait_recv()
    v["ph_half"][...] = v["ph_in"][rows(base, 512)] + v["ph_core"][...]
    scattered = []
    for step in range(1, 16):
        there = lax.rem(plane + step, 16)
        scattered.append(
            copies(v["ph_half"].at[rows(there * 32, 32)], v["ph_plane"].at[step], plane_device(step))
        )

    loads["w_query"].wait()

    @pl.loop(0, BLOCKS)
    def _(block):
        where = rows(block * BLOCK, BLOCK)
        query = dot(v["hid"][where], v["w_query"][...])
        for pair in range(PAIRS):
            part = query[:, pair * 128 : pair * 128 + 128]
            factor = lax.rsqrt(head_mean(part * part) + 1e-06)
            v["q_r"][pair, where] = factor
            v["q_n"][pair, where] = (part * factor).astype(BF16)

    own = pl.multiple_of(plane * 32, 32)
    for made in scattered:
        made.wait_recv()
    total = v["ph_half"][pl.ds(own, 32)]
    for step in range(1, 16):
        total = total + v["ph_plane"][step]
    v["ph_x"][here["x"]] = total
    mine = v["ph_x"].at[here["x"]]
    shares = [copies(mine, mine, moved(here, x=step)) for step in (2, 1, 3)]

    @pl.loop(0, 4)
    def _(part):
        where = rows(part * 256, 256)
        v["series_t"][where] = v["series"][:, where].T

    for made in shares:
        made.wait_recv()
    whole = (v["ph_x"][0] + v["ph_x"][1]) + (v["ph_x"][2] + v["ph_x"][3])
    mine = v["ph"].at[rows(base + own, 32)]
    mine[...] = whole
    spread = [copies(mine, mine, plane_device(step)) for step in range(1, 16)]
    passed = [copies(mine, mine, moved(here, c=1))]

    @pl.loop(4, 8)
    def _(part):
        where = rows(part * 256, 256)
        v["series_t"][where] = v["series"][:, where].T

    v["hid_t"][...] = v["hid"][...].T

    for step in range(1, 16):
        spread[step - 1].wait_recv()
        origin = lax.rem(plane + 16 - step, 16)
        piece = v["ph"].at[rows(base + origin * 32, 32)]
        passed.append(copies(piece, piece, moved(here, c=1)))

    @pl.loop(0, 8)
    def _(part):
        got = dot_t(v["series_t"][rows(part * 256, 256)], v["proj"][...])
        unit = lax.div(part, 4) * 2
        where = rows(lax.rem(part, 4) * 256, 256)
        sum_s.data[unit, where] = got[:, :128]
        sum_s.data[unit + 1, where] = got[:, 128:]

    for made in passed:
        made.wait_recv()
    for group in range(3):
        sum_s.core(group)

    loads["w_key"].wait()
    loads["w_value"].wait()
    ph = jnp.concatenate([v["ph"][pl.ds(pair * 256, 256)] for pair in range(PAIRS)], 1)
    ph_hi, ph_lo = hi_lo(ph)
    low_half = lax.broadcasted_iota(jnp.int32, (256, 128), 1) < 64
    none = jnp.zeros((256, 128), BF16)
    keys = dot(ph_hi, v["w_key"][...]) + dot(ph_lo, v["w_key"][...])
    values = dot(ph_hi, v["w_value"][...]) + dot(ph_lo, v["w_value"][...])
    blank = jnp.zeros((64, 256), BF16)
    for pair in range(PAIRS):
        part = keys[:, pair * 128 : pair * 128 + 128]
        factor = lax.rsqrt(head_mean(part * part) + 1e-06)
        normed = part * factor
        v["key_n"][pair] = normed
        v["key_r"][pair] = factor
        eighth = (normed * 0.125).astype(BF16)
        v["key_out"][pair, :256] = jnp.where(low_half, eighth, none)
        v["key_out"][pair, 256:] = jnp.where(low_half, none, eighth)
        turned = eighth.T
        v["key_in"][pair, :64, :256] = turned[:64]
        v["key_in"][pair, 64:, 256:] = turned[64:]
        v["key_in"][pair, :64, 256:] = blank
        v["key_in"][pair, 64:, :256] = blank
        val_hi, val_lo = hi_lo(values[:, pair * 128 : pair * 128 + 128])
        v["val_out"][pair, :256] = jnp.where(low_half, val_hi, none)
        v["val_out"][pair, 256:] = jnp.where(low_half, none, val_hi)
        for index, value in enumerate((val_hi, val_lo)):
            turned = value.T
            at = index * 128
            v["val_in"][pair, at : at + 64, :256] = turned[:64]
            v["val_in"][pair, at + 64 : at + 128, 256:] = turned[64:]
            v["val_in"][pair, at : at + 64, 256:] = blank
            v["val_in"][pair, at + 64 : at + 128, :256] = blank

    def attention(pair):
        sums = sum_q[pair // 2].data
        first = (pair % 2) * 128
        for part in range(4):
            sums[0, pl.ds(part * 256 + first, 128)] = jnp.zeros((128, 128), F32)

        @pl.loop(0, BLOCKS)
        def _(block):
            where = rows(block * BLOCK, BLOCK)
            query = v["q_n"][pair, where]
            grad = v["g_att"][pair, where]
            scores = dot(query, v["key_in"][pair])
            grad_probs = dot(jnp.concatenate([grad, grad], 1), v["val_in"][pair])
            query_t, grad_t = query.T, grad.T
            probs_b, grad_scores = [], []
            for head in range(2):
                lanes = slice(head * 256, head * 256 + 256)
                expo = jnp.exp(scores[:, lanes])
                probs = expo * (1.0 / jnp.sum(expo, axis=1, keepdims=True))
                grad_p = grad_probs[:, lanes]
                inner = jnp.sum(probs * grad_p, axis=1, keepdims=True)
                probs_b.append(probs.astype(BF16))
                grad_scores.append((probs * (grad_p - inner)).astype(BF16))
                for at, got in (
                    (0, dot(query_t[head * 64 : head * 64 + 64], grad_scores[head])),
                    (512, dot(grad_t[head * 64 : head * 64 + 64], probs_b[head])),
                ):
                    for side in range(2):
                        rest = pl.ds(at + side * 256 + first + head * 64, 64)
                        sums[0, rest] = sums[0, rest] + got[:, side * 128 : side * 128 + 128]
            attended = dot(jnp.concatenate(probs_b, 1), v["val_out"][pair])
            v["att"][pair, where] = attended.astype(BF16)
            grad_n = dot(jnp.concatenate(grad_scores, 1), v["key_out"][pair])
            normed = query.astype(F32)
            grad_q = v["q_r"][pair, where] * (grad_n - normed * head_mean(grad_n * normed))
            v["g_query"][pair, where] = grad_q.astype(BF16)

    def weight_grads(quad):
        both = (2 * quad, 2 * quad + 1)
        sums = sum_q[quad].data
        att = jnp.concatenate([v["att"][pair] for pair in both], 1)
        got = dot(att.T, v["cot"][...])
        for part in range(4):
            sums[2, pl.ds(part * 256, 256)] = got[:, part * 128 : part * 128 + 128]
        sum_q[quad].core(0)
        got = dot(v["hid_t"][...], jnp.concatenate([v["g_query"][pair] for pair in both], 1))
        for part in range(2):
            sums[1, pl.ds(part * 512, 512)] = got[:, part * 128 : part * 128 + 128]
        sum_q[quad].core(1)
        sum_q[quad].core(2)

    attention(0)
    sum_s.step1()
    attention(1)
    sum_s.step2()
    weight_grads(0)
    sum_s.step3()
    attention(2)
    sum_q[0].step1()
    sum_s.step4()
    attention(3)
    sum_q[0].step2()
    sum_s.step5()

    @pl.loop(0, BLOCKS)
    def _(block):
        where = rows(block * BLOCK, BLOCK)
        grad = jnp.concatenate([v["g_query"][pair, where] for pair in range(PAIRS)], 1)
        v["g_hid"][where] = (
            v["cot"][where].astype(F32) + dot_t(grad, v["w_query"][...])
        ).astype(BF16)

    weight_grads(1)
    sum_q[0].step3()
    sum_s.step6()

    def embed_part(index):
        @pl.loop(0, 4)
        def _(part):
            got = dot(v["series_t"][rows(index * 1024 + part * 256, 256)], v["g_hid"][...])
            where = rows(part * 256, 256)
            for unit in range(4):
                sum_e[index].data[unit, where] = got[:, unit * 128 : unit * 128 + 128]

        for group in range(3):
            sum_e[index].core(group)

    embed_part(0)
    sum_q[1].step1()
    embed_part(1)
    sum_e[0].step1()
    sum_q[0].step4()
    sum_s.step7()
    sum_q[1].step2()
    sum_e[1].step1()
    sum_q[0].step5()
    sum_q[1].step3()
    sum_e[0].step2()

    @pl.loop(0, BLOCKS)
    def _(block):
        where = rows(block * BLOCK, BLOCK)
        att = jnp.concatenate([v["att"][pair, where] for pair in range(PAIRS)], 1)
        v["out"][where] = (v["hid"][where].astype(F32) + dot(att, v["w_out"][...])).astype(BF16)

    stores = []

    def store(src, dst):
        made = pltpu.make_async_copy(src, dst, store_sem.at[len(stores)])
        made.start()
        stores.append(made)

    store(v["out"], out_hbm)
    sum_q[0].step6()
    sum_q[1].step4()
    sum_e[1].step2()
    sum_e[0].step3()
    sum_q[1].step5()
    sum_q[0].step7()
    sum_e[1].step3()
    sum_e[0].step4()
    sum_q[1].step6()
    sum_e[1].step4()
    sum_e[0].step5()
    sum_q[0].all8()
    sum_s.all8()
    sum_q[1].step7()
    sum_e[1].step5()
    sum_e[0].step6()
    for side, part in enumerate(hi_lo(ph)):
        v["ph_t"][side] = part.T
    sum_e[1].step6()
    sum_q[1].all8()
    copies.drain()

    for quad in range(2):
        for half in range(2):
            pair = quad * 2 + half
            lanes = pl.ds(pair * 128, 128)
            turned = []
            for at in (0, 512):
                turned.append(
                    jnp.concatenate(
                        [
                            sum_q[quad].out[0, pl.ds(at + side * 256 + half * 128, 128)]
                            for side in range(2)
                        ],
                        1,
                    ).T
                )
            grad_n = turned[0] * 0.125
            normed = v["key_n"][pair]
            grad_k = v["key_r"][pair] * (grad_n - normed * head_mean(grad_n * normed))
            for index, (name, value) in enumerate((("gk", grad_k), ("gv", turned[1]))):
                for side, part in enumerate(hi_lo(value)):
                    v[name][side, :, lanes] = part
    back = dot_t(v["gk"][0], v["w_key"][...]) + dot_t(v["gk"][1], v["w_key"][...])
    back = back + dot_t(v["gv"][0], v["w_value"][...]) + dot_t(v["gv"][1], v["w_value"][...])
    for side, part in enumerate(hi_lo(back)):
        v["back"][side] = part
    for index, name in enumerate(("gk", "gv")):
        got = dot(v["ph_t"][0], v[name][0]) + dot(v["ph_t"][0], v[name][1])
        got = (got + dot(v["ph_t"][1], v[name][0])) * NORM
        for part in range(4):
            sum_s.data[
                index * 2 + part // 2, pl.ds((part % 2) * 512, 512)
            ] = got[:, part * 128 : part * 128 + 128]
            store(
                sum_s.data.at[index * 2 + part // 2, pl.ds((part % 2) * 512, 512)],
                attn_hbm.at[1 + index, :, pl.ds(part * 128, 128)],
            )
    for quad in range(2):
        out = sum_q[quad].out

        @pl.loop(1, 3)
        def _(unit):
            out[unit] = out[unit] * NORM

        for part in range(2):
            store(
                out.at[1, pl.ds(part * 512, 512)],
                attn_hbm.at[0, :, pl.ds(quad * 256 + part * 128, 128)],
            )
        for part in range(4):
            store(
                out.at[2, pl.ds(part * 256, 256)],
                attn_hbm.at[3, pl.ds(quad * 256, 256), pl.ds(part * 128, 128)],
            )
    sum_e[0].step7()
    sum_e[1].step7()
    for index in range(2):

        @pl.loop(0, 4)
        def _(part):
            where = rows(part * 256, 256)
            left = jnp.concatenate([sum_s.out[index * 2 + side, where] for side in range(2)], 1)
            left_hi, left_lo = hi_lo(left)
            got = dot(left_hi, v["back"][0]) + dot(left_hi, v["back"][1])
            got = got + dot(left_lo, v["back"][0])
            for unit in range(4):
                sum_e[index].data[unit, where] = got[:, unit * 128 : unit * 128 + 128]

    for index in range(2):
        for group, (_, start, size) in enumerate(E_GROUPS[index]):
            sum_e[index].step8(group)
            if group == 2:
                copies.drain()
        for unit in range(4):

            @pl.loop(0, 4)
            def _(part):
                where = (unit, rows(part * 256, 256))
                sum_e[index].out[where] = (
                    sum_e[index].out[where] + sum_e[index].data[where]
                ) * NORM

            store(
                sum_e[index].out.at[unit],
                embed_hbm.at[pl.ds(index * 1024, 1024), pl.ds(unit * 128, 128)],
            )
    copies.drain()
    for made in stores:
        made.wait()


def local(series, w_embed, w_query, w_key, w_value, w_out, proj, cotangent):
    anywhere = pl.BlockSpec(memory_space=pl.ANY)
    return pl.pallas_call(
        layer_kernel,
        out_shape=(
            jax.ShapeDtypeStruct((ROWS, WIDTH), BF16),
            jax.ShapeDtypeStruct((LOOKBACK, WIDTH), F32),
            jax.ShapeDtypeStruct((4, WIDTH, WIDTH), F32),
        ),
        in_specs=[anywhere] * 8,
        out_specs=(anywhere,) * 3,
        scratch_shapes=[VMEM(shape, dtype) for shape, dtype in SHAPES.values()]
        + sum_bufs(4)
        + sum_bufs(3) * 2
        + sum_bufs(4) * 2
        + [
            pltpu.SemaphoreType.DMA((N_COPIES,)),
            pltpu.SemaphoreType.DMA((N_COPIES,)),
            pltpu.SemaphoreType.DMA((len(LOADS) + BLOCKS,)),
            pltpu.SemaphoreType.DMA((32,)),
        ],
        compiler_params=pltpu.CompilerParams(
            collective_id=0, has_side_effects=True, vmem_limit_bytes=63 * 1024 * 1024
        ),
    )(series, w_embed, w_query, w_key, w_value, w_out, proj, cotangent)


def solution(mesh):
    return jax.shard_map(
        local,
        mesh=mesh,
        in_specs=(
            P(("var", "grp"), None),
            P(),
            P(),
            P(),
            P(),
            P(),
            P(None, ("var", "grp")),
            P(("var", "grp"), None),
        ),
        out_specs=(P(("var", "grp"), None), P(), P()),
        check_vma=False,
    )
```

```python
import functools
import math

import jax
import jax.numpy as jnp
from jax import lax
from jax.experimental import pallas as pl
from jax.experimental.pallas import tpu as pltpu
from jax.sharding import PartitionSpec as P

MESH = pl.DeviceIdType.MESH
F32 = jnp.float32
BF16 = jnp.bfloat16
VMEM = pltpu.VMEM
ROWS = 1024
WIDTH = 512
LOOKBACK = 2048
KP = 256
PAIRS = 4
BLOCK = 256
BLOCKS = ROWS // BLOCK
NORM = 1.0 / math.sqrt(131072.0)


def dot(left, right, dims=((1,), (0,))):
    return lax.dot_general(left, right, (dims, ((), ())), preferred_element_type=F32)


def dot_t(left, right):
    return dot(left, right, ((1,), (1,)))


def hi_lo(values):
    upper = values.astype(BF16)
    return upper, (values - upper.astype(F32)).astype(BF16)


def rows(start, size, step=None):
    return pl.ds(pl.multiple_of(start, step or size), size)


def position():
    var = lax.axis_index("var")
    return {
        "x": lax.div(var, 8),
        "y": lax.rem(lax.div(var, 2), 4),
        "c": lax.rem(var, 2),
        "z": lax.axis_index("grp"),
    }


def moved(place, **steps):
    there = dict(place)
    for axis, step in steps.items():
        there[axis] = lax.rem(place[axis] + step, 2 if axis == "c" else 4)
    return (there["x"] * 8 + there["y"] * 2 + there["c"], there["z"])


class Copies:
    def __init__(self, send, recv):
        self.send, self.recv = send, recv
        self.count = 0
        self.waiting = []

    def __call__(self, src, dst, device):
        slot = self.count
        self.count += 1
        made = pltpu.make_async_remote_copy(
            src_ref=src,
            dst_ref=dst,
            send_sem=self.send.at[slot],
            recv_sem=self.recv.at[slot],
            device_id=device,
            device_id_type=MESH,
        )
        made.start()
        self.waiting.append(made)
        return made

    def drain(self, first=None):
        for made in self.waiting[:first]:
            made.wait_send()
        self.waiting = self.waiting[len(self.waiting) if first is None else first :]


X, Y, Z = ("x", "y", "z"), ("y", "z", "x"), ("z", "x", "y")


class Sum:
    def __init__(self, here, copies, groups, bufs):
        self.here, self.copy, self.groups = here, copies, groups
        self.data, self.half, self.one, self.two, self.three, self.out = bufs
        self.base = here["c"] * 512
        self.across = []
        self.made = {}
        self.sends = []

    def core(self, group):
        _, start, size = self.groups[group]
        units = pl.ds(start, size)
        self.across.append(
            self.copy(
                self.data.at[units, rows((1 - self.here["c"]) * 512, 512)],
                self.half.at[units],
                moved(self.here, c=1),
            )
        )
        self.sends.append(self.across[-1])

    def place(self, group, level):
        order = self.groups[group][0]
        sizes = (128, 32)
        at = self.base
        for axis, size in zip(order[:level], sizes[:level]):
            at = at + self.here[axis] * size
        return at

    def scatter(self, level, group):
        order, start, size = self.groups[group]
        axis = order[level]
        extent = (128, 32)[level]
        buffer = (self.one, self.two)[level]
        at = self.place(group, level)
        self.made[group] = [
            self.copy(
                self.data.at[
                    pl.ds(start, size),
                    rows(at + lax.rem(self.here[axis] + step, 4) * extent, extent),
                ],
                buffer.at[step - 1, pl.ds(start, size)],
                moved(self.here, **{axis: step}),
            )
            for step in (2, 1, 3)
        ]
        self.sends += self.made[group]

    def settle(self):
        for made in self.sends:
            made.wait_send()
        self.copy.waiting = [
            made for made in self.copy.waiting if not any(made is one for one in self.sends)
        ]

    def gather(self, level, group):
        order, start, size = self.groups[group]
        axis = order[level]
        extent = (128, 32)[level]
        own = self.out.at[pl.ds(start, size), rows(self.place(group, level + 1), extent)]
        self.made[group] = [
            self.copy(own, own, moved(self.here, **{axis: step})) for step in (2, 1, 3)
        ]
        return own

    def step1(self):
        for group, (_, start, size) in enumerate(self.groups):
            self.across[group].wait_recv()

            @pl.loop(start, start + size)
            def _(unit):
                where = (unit, rows(self.base, 512))
                self.data[where] = self.data[where] + self.half[unit]

            self.scatter(0, group)

    def reduced(self, level, group):
        order, start, size = self.groups[group]
        extent = (128, 32)[level]
        buffer = (self.one, self.two)[level]
        for made in self.made[group]:
            made.wait_recv()
        units = pl.ds(start, size)
        where = (units, rows(self.place(group, level + 1), extent))
        total = (self.data[where] + buffer[0, units]) + (buffer[1, units] + buffer[2, units])
        if level == 0:
            self.data[where] = total
        else:
            mine = (self.here[order[2]], units)
            self.three[mine] = total
            self.made[group] = [
                self.copy(
                    self.three.at[mine],
                    self.three.at[mine],
                    moved(self.here, **{order[2]: step}),
                )
                for step in (2, 1, 3)
            ]

    def step2(self):
        for group in range(len(self.groups)):
            self.reduced(0, group)
            self.scatter(1, group)

    def step3(self):
        for group in range(len(self.groups)):
            self.reduced(1, group)

    def step4(self):
        for group, (_, start, size) in enumerate(self.groups):
            self.gathered(group)
            units = pl.ds(start, size)
            part = [self.three[index, units] for index in range(4)]
            where = (units, rows(self.place(group, 2), 32))
            self.out[where] = (part[0] + part[1]) + (part[2] + part[3])
            self.gather(1, group)

    def gathered(self, group):
        for made in self.made[group]:
            made.wait_recv()

    def step5(self):
        self.passed = []
        for group in range(len(self.groups)):
            self.gathered(group)
            own = self.gather(0, group)
            self.passed.append([self.copy(own, own, moved(self.here, c=1))])

    def step6(self):
        for group, (order, start, size) in enumerate(self.groups):
            for made, step in zip(self.made[group], (2, 1, 3)):
                made.wait_recv()
                chunk = lax.rem(self.here[order[0]] + 4 - step, 4)
                piece = self.out.at[pl.ds(start, size), rows(self.base + chunk * 128, 128)]
                self.passed[group].append(self.copy(piece, piece, moved(self.here, c=1)))

    def step7(self, group):
        for made in self.passed[group]:
            made.wait_recv()

    def all7(self):
        for group in range(len(self.groups)):
            self.step7(group)


def sum_bufs(units, out=True):
    return [
        VMEM((units, 1024, 128), F32),
        VMEM((units, 512, 128), F32),
        VMEM((3, units, 128, 128), F32),
        VMEM((3, units, 32, 128), F32),
        VMEM((4, units, 32, 128), F32),
    ] + [VMEM((units, 1024, 128), F32)] * out


S_GROUPS = ((X, 0, 1), (Y, 1, 2), (Z, 3, 1))
Q_GROUPS = ((X, 0, 1), (Y, 1, 1), (Z, 2, 1))
E_GROUPS = (((X, 0, 2), (Y, 2, 1), (Z, 3, 1)), ((Z, 0, 2), (Y, 2, 1), (X, 3, 1)))

SHAPES = dict(
    series=((ROWS, LOOKBACK), BF16),
    w_embed=((LOOKBACK, WIDTH), BF16),
    w_query=((WIDTH, WIDTH), BF16),
    w_key=((WIDTH, WIDTH), BF16),
    w_value=((WIDTH, WIDTH), BF16),
    w_out=((WIDTH, WIDTH), BF16),
    proj=((KP, ROWS), BF16),
    cot=((ROWS, WIDTH), BF16),
    series_t=((LOOKBACK, ROWS), BF16),
    hid=((ROWS, WIDTH), BF16),
    hid_t=((WIDTH, ROWS), BF16),
    key_n=((PAIRS, KP, 128), F32),
    key_r=((PAIRS, KP, 128), F32),
    key_in=((PAIRS, 128, 512), BF16),
    key_out=((PAIRS, 512, 128), BF16),
    val_in=((PAIRS, 256, 512), BF16),
    val_out=((PAIRS, 512, 128), BF16),
    ph_core=((512, 128), F32),
    ph_plane=((16, 32, 128), F32),
    ph_x=((4, 32, 128), F32),
    ph=((1024, 128), F32),
)
LOADS = ("w_embed", "proj", "w_query", "cot", "w_out", "w_key", "w_value")
N_COPIES = 50 + 5 * 3 * 20


def layer_kernel(*refs):
    names = ("series", "w_embed", "w_query", "w_key", "w_value", "w_out", "proj", "cot")
    hbm = dict(zip(names, refs[:8]))
    out_hbm, embed_hbm, attn_hbm = refs[8:11]
    refs = refs[11:]
    v = dict(zip(SHAPES, refs[: len(SHAPES)]))
    for slot, name in enumerate(("att", "g_query", "g_hid", "out")):
        v[name] = v["series"].at[:, pl.ds(slot * WIDTH, WIDTH)]
    for slot, name in enumerate(("q_n", "g_att")):
        v[name] = v["w_embed"].at[pl.ds(slot * ROWS, ROWS)]
    refs = refs[len(SHAPES) :]
    s_bufs, q0_bufs, q1_bufs, e1_bufs = (refs[6 * i : 6 * i + 6] for i in range(4))
    e0_bufs = refs[24:29] + (s_bufs[0],)
    send, recv, load_sem, store_sem = refs[29:]
    v["q_r"] = e1_bufs[0]
    v["ph_in"] = e0_bufs[0].at[0]
    v["ph_half"] = e0_bufs[0].at[1, pl.ds(0, 512)]
    for side in range(2):
        where = pl.ds(side * KP, KP)
        v["gk", side] = v["hid_t"].at[where, pl.ds(0, WIDTH)]
        v["gv", side] = v["hid_t"].at[where, pl.ds(WIDTH, WIDTH)]
        v["back", side] = v["g_query"].at[where]
        v["ph_t", side] = v["g_hid"].at[pl.ds(0, WIDTH), pl.ds(side * KP, KP)]
    here = position()
    core, plane = here["c"], here["y"] * 4 + here["z"]
    base = core * 512

    def plane_device(step):
        there = lax.rem(plane + step, 16)
        return (here["x"] * 8 + lax.div(there, 4) * 2 + core, lax.rem(there, 4))

    loads = {}
    for slot, name in enumerate(LOADS):
        loads[name] = pltpu.make_async_copy(hbm[name], v[name], load_sem.at[slot])
    series_loads = []
    for block in range(BLOCKS):
        where = pl.ds(block * BLOCK, BLOCK)
        series_loads.append(
            pltpu.make_async_copy(
                hbm["series"].at[where], v["series"].at[where], load_sem.at[len(LOADS) + block]
            )
        )
    loads["w_embed"].start()
    for made in series_loads:
        made.start()
    loads["proj"].start()

    barrier = pltpu.get_barrier_semaphore()
    others = [moved(here, c=1)]
    others += [moved(here, x=step) for step in (1, 2, 3)]
    others += [plane_device(step) for step in range(1, 16)]
    for device in others:
        pl.semaphore_signal(barrier, inc=1, device_id=device, device_id_type=MESH)

    copies = Copies(send, recv)
    sum_s = Sum(here, copies, S_GROUPS, s_bufs)
    sum_q = [Sum(here, copies, Q_GROUPS, bufs) for bufs in (q0_bufs, q1_bufs)]
    sum_e = [Sum(here, copies, E_GROUPS[i], bufs) for i, bufs in enumerate((e0_bufs, e1_bufs))]

    lane = lax.broadcasted_iota(jnp.int32, (256, 128), 1) & 64
    row = lax.broadcasted_iota(jnp.int32, (256, 128), 0) & 64
    ones = jnp.where(lane == row, 1.0 / 64, 0.0).astype(BF16)

    def head_mean(values):
        return dot(jnp.concatenate(hi_lo(values), 1), ones)

    loads["w_embed"].wait()
    for block in range(BLOCKS):
        series_loads[block].wait()
        if block == 2:
            for name in LOADS[2:]:
                loads[name].start()
        where = pl.ds(block * BLOCK, BLOCK)
        v["hid"][where] = dot(v["series"][where], v["w_embed"][...]).astype(BF16)
    loads["proj"].wait()
    part = dot(v["proj"][...], v["hid"][...])
    for pair in range(PAIRS):
        v["ph_in"][pl.ds(pair * 256, 256)] = part[:, pair * 128 : pair * 128 + 128]

    pl.semaphore_wait(barrier, len(others))
    across = copies(v["ph_in"].at[rows((1 - core) * 512, 512)], v["ph_core"], moved(here, c=1))

    loads["w_query"].wait()

    @pl.loop(0, BLOCKS)
    def _(block):
        where = rows(block * BLOCK, BLOCK)
        query = dot(v["hid"][where], v["w_query"][...])
        for pair in range(PAIRS):
            part = query[:, pair * 128 : pair * 128 + 128]
            factor = lax.rsqrt(head_mean(part * part) + 1e-06)
            v["q_r"][pair, where] = factor
            v["q_n"][where, pl.ds(pair * 128, 128)] = (part * factor).astype(BF16)

    across.wait_recv()
    v["ph_half"][...] = v["ph_in"][rows(base, 512)] + v["ph_core"][...]
    scattered = []
    for step in range(1, 16):
        there = lax.rem(plane + step, 16)
        scattered.append(
            copies(v["ph_half"].at[rows(there * 32, 32)], v["ph_plane"].at[step], plane_device(step))
        )

    @pl.loop(0, 8)
    def _(part):
        where = rows(part * 256, 256)
        v["series_t"][where] = v["series"][:, where].T

    own = pl.multiple_of(plane * 32, 32)
    @pl.loop(0, 8)
    def _(part):
        got = dot_t(v["series_t"][rows(part * 256, 256)], v["proj"][...])
        unit = lax.div(part, 4) * 2
        where = rows(lax.rem(part, 4) * 256, 256)
        sum_s.data[unit, where] = got[:, :128]
        sum_s.data[unit + 1, where] = got[:, 128:]

    for made in scattered:
        made.wait_recv()
    total = v["ph_half"][pl.ds(own, 32)]
    for step in range(1, 16):
        total = total + v["ph_plane"][step]
    v["ph_x"][here["x"]] = total
    mine = v["ph_x"].at[here["x"]]
    shares = [copies(mine, mine, moved(here, x=step)) for step in (2, 1, 3)]
    for group in range(3):
        sum_s.core(group)

    loads["cot"].wait()
    loads["w_out"].wait()

    @pl.loop(0, BLOCKS)
    def _(block):
        where = rows(block * BLOCK, BLOCK)
        grad = dot_t(v["cot"][where], v["w_out"][...]).astype(BF16)
        v["g_att"][where] = grad

    for made in shares:
        made.wait_recv()
    whole = (v["ph_x"][0] + v["ph_x"][1]) + (v["ph_x"][2] + v["ph_x"][3])
    mine = v["ph"].at[rows(base + own, 32)]
    mine[...] = whole
    spread = [copies(mine, mine, plane_device(step)) for step in range(1, 16)]
    passed = [copies(mine, mine, moved(here, c=1))]
    sum_s.step1()
    v["hid_t"][...] = v["hid"][...].T

    for step in range(1, 16):
        spread[step - 1].wait_recv()
        origin = lax.rem(plane + 16 - step, 16)
        piece = v["ph"].at[rows(base + origin * 32, 32)]
        passed.append(copies(piece, piece, moved(here, c=1)))

    for made in passed:
        made.wait_recv()
    copies.drain(16)

    loads["w_key"].wait()
    loads["w_value"].wait()
    ph = jnp.concatenate([v["ph"][pl.ds(pair * 256, 256)] for pair in range(PAIRS)], 1)
    ph_hi, ph_lo = hi_lo(ph)
    low_half = lax.broadcasted_iota(jnp.int32, (256, 128), 1) < 64
    none = jnp.zeros((256, 128), BF16)
    keys = dot(ph_hi, v["w_key"][...]) + dot(ph_lo, v["w_key"][...])
    values = dot(ph_hi, v["w_value"][...]) + dot(ph_lo, v["w_value"][...])
    blank = jnp.zeros((64, 256), BF16)
    for pair in range(PAIRS):
        part = keys[:, pair * 128 : pair * 128 + 128]
        factor = lax.rsqrt(head_mean(part * part) + 1e-06)
        normed = part * factor
        v["key_n"][pair] = normed
        v["key_r"][pair] = factor
        eighth = (normed * 0.125).astype(BF16)
        v["key_out"][pair, :256] = jnp.where(low_half, eighth, none)
        v["key_out"][pair, 256:] = jnp.where(low_half, none, eighth)
        turned = eighth.T
        v["key_in"][pair, :64, :256] = turned[:64]
        v["key_in"][pair, 64:, 256:] = turned[64:]
        v["key_in"][pair, :64, 256:] = blank
        v["key_in"][pair, 64:, :256] = blank
        val_hi, val_lo = hi_lo(values[:, pair * 128 : pair * 128 + 128])
        v["val_out"][pair, :256] = jnp.where(low_half, val_hi, none)
        v["val_out"][pair, 256:] = jnp.where(low_half, none, val_hi)
        for index, value in enumerate((val_hi, val_lo)):
            turned = value.T
            at = index * 128
            v["val_in"][pair, at : at + 64, :256] = turned[:64]
            v["val_in"][pair, at + 64 : at + 128, 256:] = turned[64:]
            v["val_in"][pair, at : at + 64, 256:] = blank
            v["val_in"][pair, at + 64 : at + 128, :256] = blank

    def attention(pair):
        sums = sum_q[pair // 2].data
        first = (pair % 2) * 128
        lanes_of = pl.ds(pair * 128, 128)
        for part in range(4):
            sums[0, pl.ds(part * 256 + first, 128)] = jnp.zeros((128, 128), F32)

        @pl.loop(0, BLOCKS)
        def _(block):
            where = rows(block * BLOCK, BLOCK)
            query = v["q_n"][where, lanes_of]
            grad = v["g_att"][where, lanes_of]
            scores = dot(query, v["key_in"][pair])
            grad_probs = dot(jnp.concatenate([grad, grad], 1), v["val_in"][pair])
            query_t, grad_t = query.T, grad.T
            probs_b, grad_scores = [], []
            for head in range(2):
                lanes = slice(head * 256, head * 256 + 256)
                expo = jnp.exp(scores[:, lanes])
                probs = expo * (1.0 / jnp.sum(expo, axis=1, keepdims=True))
                grad_p = grad_probs[:, lanes]
                inner = jnp.sum(probs * grad_p, axis=1, keepdims=True)
                probs_b.append(probs.astype(BF16))
                grad_scores.append((probs * (grad_p - inner)).astype(BF16))
                for at, got in (
                    (0, dot(query_t[head * 64 : head * 64 + 64], grad_scores[head])),
                    (512, dot(grad_t[head * 64 : head * 64 + 64], probs_b[head])),
                ):
                    for side in range(2):
                        rest = pl.ds(at + side * 256 + first + head * 64, 64)
                        sums[0, rest] = sums[0, rest] + got[:, side * 128 : side * 128 + 128]
            attended = dot(jnp.concatenate(probs_b, 1), v["val_out"][pair])
            v["att"][where, lanes_of] = attended.astype(BF16)
            grad_n = dot(jnp.concatenate(grad_scores, 1), v["key_out"][pair])
            normed = query.astype(F32)
            grad_q = v["q_r"][pair, where] * (grad_n - normed * head_mean(grad_n * normed))
            v["g_query"][where, lanes_of] = grad_q.astype(BF16)

    def weight_grads(quad):
        both = pl.ds(quad * 256, 256)
        sums = sum_q[quad].data
        got = dot(v["att"][:, both].T, v["cot"][...])
        for part in range(4):
            sums[2, pl.ds(part * 256, 256)] = got[:, part * 128 : part * 128 + 128]
        sum_q[quad].core(0)
        got = dot(v["hid_t"][...], v["g_query"][:, both])
        for part in range(2):
            sums[1, pl.ds(part * 512, 512)] = got[:, part * 128 : part * 128 + 128]
        sum_q[quad].core(1)
        sum_q[quad].core(2)

    attention(0)
    sum_s.step2()
    attention(1)
    weight_grads(0)
    sum_s.step3()
    attention(2)
    sum_q[0].step1()
    sum_s.step4()
    attention(3)
    sum_q[0].step2()
    sum_s.step5()

    @pl.loop(0, BLOCKS)
    def _(block):
        where = rows(block * BLOCK, BLOCK)
        v["g_hid"][where] = (
            v["cot"][where].astype(F32) + dot_t(v["g_query"][where], v["w_query"][...])
        ).astype(BF16)

    weight_grads(1)
    sum_q[0].step3()

    def embed_part(index):
        @pl.loop(0, 4)
        def _(part):
            got = dot(v["series_t"][rows(index * 1024 + part * 256, 256)], v["g_hid"][...])
            where = rows(part * 256, 256)
            for unit in range(4):
                sum_e[index].data[unit, where] = got[:, unit * 128 : unit * 128 + 128]

        for group in range(3):
            sum_e[index].core(group)

    sum_s.settle()
    embed_part(0)
    sum_q[1].step1()
    embed_part(1)
    sum_e[0].step1()
    sum_q[0].step4()
    sum_s.step6()
    sum_e[1].step1()
    sum_q[1].step2()

    @pl.loop(0, BLOCKS)
    def _(block):
        where = rows(block * BLOCK, BLOCK)
        v["out"][where] = (
            v["hid"][where].astype(F32) + dot(v["att"][where], v["w_out"][...])
        ).astype(BF16)

    stores = []

    def store(src, dst):
        made = pltpu.make_async_copy(src, dst, store_sem.at[len(stores)])
        made.start()
        stores.append(made)

    store(v["out"], out_hbm)
    sum_e[0].step2()
    sum_q[0].step5()
    sum_q[1].step3()
    sum_e[1].step2()
    sum_e[0].step3()
    sum_q[1].step4()
    sum_q[0].step6()
    sum_e[1].step3()
    sum_e[0].step4()
    sum_q[1].step5()
    sum_e[1].step4()
    sum_e[0].step5()
    sum_q[0].all7()
    sum_s.all7()
    for side, part in enumerate(hi_lo(ph)):
        v["ph_t", side][...] = part.T
    sum_q[1].step6()
    sum_e[1].step5()
    sum_q[1].all7()
    copies.drain()

    for quad in range(2):
        for half in range(2):
            pair = quad * 2 + half
            lanes = pl.ds(pair * 128, 128)
            turned = []
            for at in (0, 512):
                turned.append(
                    jnp.concatenate(
                        [
                            sum_q[quad].out[0, pl.ds(at + side * 256 + half * 128, 128)]
                            for side in range(2)
                        ],
                        1,
                    ).T
                )
            grad_n = turned[0] * 0.125
            normed = v["key_n"][pair]
            grad_k = v["key_r"][pair] * (grad_n - normed * head_mean(grad_n * normed))
            for index, (name, value) in enumerate((("gk", grad_k), ("gv", turned[1]))):
                for side, part in enumerate(hi_lo(value)):
                    v[name, side][:, lanes] = part
    back = dot_t(v["gk", 0][...], v["w_key"][...]) + dot_t(v["gk", 1][...], v["w_key"][...])
    back = back + dot_t(v["gv", 0][...], v["w_value"][...]) + dot_t(v["gv", 1][...], v["w_value"][...])
    for side, part in enumerate(hi_lo(back)):
        v["back", side][...] = part
    for index, name in enumerate(("gk", "gv")):
        got = dot(v["ph_t", 0][...], v[name, 0][...]) + dot(v["ph_t", 0][...], v[name, 1][...])
        got = (got + dot(v["ph_t", 1][...], v[name, 0][...])) * NORM
        for part in range(4):
            where = (part // 2, pl.ds((part % 2) * 512, 512))
            sum_q[index].data[where] = got[:, part * 128 : part * 128 + 128]
            store(sum_q[index].data.at[where], attn_hbm.at[1 + index, :, pl.ds(part * 128, 128)])
    for quad in range(2):
        out = sum_q[quad].out

        @pl.loop(1, 3)
        def _(unit):
            out[unit] = out[unit] * NORM

        for part in range(2):
            store(
                out.at[1, pl.ds(part * 512, 512)],
                attn_hbm.at[0, :, pl.ds(quad * 256 + part * 128, 128)],
            )
        for part in range(4):
            store(
                out.at[2, pl.ds(part * 256, 256)],
                attn_hbm.at[3, pl.ds(quad * 256, 256), pl.ds(part * 128, 128)],
            )
    sum_e[0].step6()
    sum_e[1].step6()
    for index in range(2):

        @pl.loop(0, 4)
        def _(part):
            where = rows(part * 256, 256)
            left = jnp.concatenate([sum_s.out[index * 2 + side, where] for side in range(2)], 1)
            left_hi, left_lo = hi_lo(left)
            got = dot(left_hi, v["back", 0][...]) + dot(left_hi, v["back", 1][...])
            got = got + dot(left_lo, v["back", 0][...])
            for unit in range(4):
                sum_e[index].data[unit, where] = got[:, unit * 128 : unit * 128 + 128]

    for index in range(2):
        for group, (_, start, size) in enumerate(E_GROUPS[index]):
            sum_e[index].step7(group)
            if group == 2:
                copies.drain()
        for unit in range(4):

            @pl.loop(0, 4)
            def _(part):
                where = (unit, rows(part * 256, 256))
                sum_e[index].out[where] = (
                    sum_e[index].out[where] + sum_e[index].data[where]
                ) * NORM

            store(
                sum_e[index].out.at[unit],
                embed_hbm.at[pl.ds(index * 1024, 1024), pl.ds(unit * 128, 128)],
            )
    copies.drain()
    for made in stores:
        made.wait()


def local(series, w_embed, w_query, w_key, w_value, w_out, proj, cotangent):
    anywhere = pl.BlockSpec(memory_space=pl.ANY)
    return pl.pallas_call(
        layer_kernel,
        out_shape=(
            jax.ShapeDtypeStruct((ROWS, WIDTH), BF16),
            jax.ShapeDtypeStruct((LOOKBACK, WIDTH), F32),
            jax.ShapeDtypeStruct((4, WIDTH, WIDTH), F32),
        ),
        in_specs=[anywhere] * 8,
        out_specs=(anywhere,) * 3,
        scratch_shapes=[VMEM(shape, dtype) for shape, dtype in SHAPES.values()]
        + sum_bufs(4)
        + sum_bufs(3) * 2
        + sum_bufs(4)
        + sum_bufs(4, False)
        + [
            pltpu.SemaphoreType.DMA((N_COPIES,)),
            pltpu.SemaphoreType.DMA((N_COPIES,)),
            pltpu.SemaphoreType.DMA((len(LOADS) + BLOCKS,)),
            pltpu.SemaphoreType.DMA((32,)),
        ],
        compiler_params=pltpu.CompilerParams(
            collective_id=0, has_side_effects=True, vmem_limit_bytes=63 * 1024 * 1024
        ),
    )(series, w_embed, w_query, w_key, w_value, w_out, proj, cotangent)


def solution(mesh):
    return jax.shard_map(
        local,
        mesh=mesh,
        in_specs=(
            P(("var", "grp"), None),
            P(),
            P(),
            P(),
            P(),
            P(),
            P(None, ("var", "grp")),
            P(("var", "grp"), None),
        ),
        out_specs=(P(("var", "grp"), None), P(), P()),
        check_vma=False,
    )
```

```python
import functools
import math

import jax
import jax.numpy as jnp
from jax import lax
from jax.experimental import pallas as pl
from jax.experimental.pallas import tpu as pltpu
from jax.sharding import PartitionSpec as P

MESH = pl.DeviceIdType.MESH
F32 = jnp.float32
BF16 = jnp.bfloat16
VMEM = pltpu.VMEM
ROWS = 1024
WIDTH = 512
LOOKBACK = 2048
KP = 256
PAIRS = 4
BLOCK = 256
BLOCKS = ROWS // BLOCK
NORM = 1.0 / math.sqrt(131072.0)


def dot(left, right, dims=((1,), (0,))):
    return lax.dot_general(left, right, (dims, ((), ())), preferred_element_type=F32)


def dot_t(left, right):
    return dot(left, right, ((1,), (1,)))


def hi_lo(values):
    upper = values.astype(BF16)
    return upper, (values - upper.astype(F32)).astype(BF16)


def rows(start, size, step=None):
    return pl.ds(pl.multiple_of(start, step or size), size)


def position():
    var = lax.axis_index("var")
    return {
        "x": lax.div(var, 8),
        "y": lax.rem(lax.div(var, 2), 4),
        "c": lax.rem(var, 2),
        "z": lax.axis_index("grp"),
    }


def moved(place, **steps):
    there = dict(place)
    for axis, step in steps.items():
        there[axis] = lax.rem(place[axis] + step, 2 if axis == "c" else 4)
    return (there["x"] * 8 + there["y"] * 2 + there["c"], there["z"])


class Batch:
    def __init__(self, pool, whole):
        slot = pool.count
        pool.count += 1
        pool.open.append(self)
        self.send, self.recv, self.whole = pool.send.at[slot], pool.recv.at[slot], whole

    def add(self, src, dst, device):
        self.device = device
        self.copy(src, dst).start()

    def copy(self, src, dst):
        return pltpu.make_async_remote_copy(
            src_ref=src,
            dst_ref=dst,
            send_sem=self.send,
            recv_sem=self.recv,
            device_id=self.device,
            device_id_type=MESH,
        )

    def wait_recv(self):
        self.copy(self.whole, self.whole).wait_recv()

    def wait_send(self):
        self.copy(self.whole, self.whole).wait_send()


class Pool:
    def __init__(self, send, recv):
        self.send, self.recv, self.count, self.open = send, recv, 0, []

    def batch(self, whole):
        return Batch(self, whole)

    def drain(self, batches=None):
        for one in list(self.open) if batches is None else batches:
            one.wait_send()
            self.open.remove(one)


X, Y, Z = ("x", "y", "z"), ("y", "z", "x"), ("z", "x", "y")


class Sum:
    def __init__(self, here, pool, groups, bufs):
        self.here, self.pool, self.groups = here, pool, groups
        self.data, self.half, self.one, self.two, self.three, self.out = bufs
        self.base = here["c"] * 512
        self.across = []
        self.made = {}
        self.passed = []
        self.sends = []
        self.batches = []

    def batch(self, whole):
        self.batches.append(self.pool.batch(whole))
        return self.batches[-1]

    def finish(self):
        self.pool.drain([one for one in self.batches if one in self.pool.open])

    def units(self, group):
        return pl.ds(self.groups[group][1], self.groups[group][2])

    def core(self, group):
        units = self.units(group)
        self.across.append(self.batch(self.half.at[units]))
        self.sends.append(self.across[-1])
        self.across[-1].add(
            self.data.at[units, rows((1 - self.here["c"]) * 512, 512)],
            self.half.at[units],
            moved(self.here, c=1),
        )

    def place(self, group, level):
        at = self.base
        for axis, size in zip(self.groups[group][0][:level], (128, 32)):
            at = at + self.here[axis] * size
        return at

    def scatter(self, level, group):
        units = self.units(group)
        axis = self.groups[group][0][level]
        extent = (128, 32)[level]
        buffer = (self.one, self.two)[level]
        at = self.place(group, level)
        self.made[group] = self.batch(buffer.at[:, units])
        self.sends.append(self.made[group])
        for step in (2, 1, 3):
            self.made[group].add(
                self.data.at[
                    units, rows(at + lax.rem(self.here[axis] + step, 4) * extent, extent)
                ],
                buffer.at[step - 1, units],
                moved(self.here, **{axis: step}),
            )

    def settle(self):
        self.pool.drain(self.sends)

    def gather(self, level, group):
        units = self.units(group)
        axis = self.groups[group][0][level]
        extent = (128, 32)[level]
        own = self.out.at[units, rows(self.place(group, level + 1), extent)]
        self.made[group] = self.batch(self.out.at[units, pl.ds(0, 3 * extent)])
        for step in (2, 1, 3):
            self.made[group].add(own, own, moved(self.here, **{axis: step}))
        return own

    def step1(self):
        for group, (_, start, size) in enumerate(self.groups):
            self.across[group].wait_recv()

            @pl.loop(start, start + size)
            def _(unit):
                where = (unit, rows(self.base, 512))
                self.data[where] = self.data[where] + self.half[unit]

            self.scatter(0, group)

    def reduced(self, level, group):
        order = self.groups[group][0]
        extent = (128, 32)[level]
        buffer = (self.one, self.two)[level]
        self.made[group].wait_recv()
        units = self.units(group)
        where = (units, rows(self.place(group, level + 1), extent))
        total = (self.data[where] + buffer[0, units]) + (buffer[1, units] + buffer[2, units])
        if level == 0:
            self.data[where] = total
        else:
            mine = (self.here[order[2]], units)
            self.three[mine] = total
            self.made[group] = self.batch(self.three.at[pl.ds(0, 3), units])
            for step in (2, 1, 3):
                self.made[group].add(
                    self.three.at[mine],
                    self.three.at[mine],
                    moved(self.here, **{order[2]: step}),
                )

    def step2(self):
        for group in range(len(self.groups)):
            self.reduced(0, group)
            self.scatter(1, group)

    def step3(self):
        for group in range(len(self.groups)):
            self.reduced(1, group)

    def step4(self):
        for group in range(len(self.groups)):
            self.made[group].wait_recv()
            units = self.units(group)
            part = [self.three[index, units] for index in range(4)]
            where = (units, rows(self.place(group, 2), 32))
            self.out[where] = (part[0] + part[1]) + (part[2] + part[3])
            self.gather(1, group)

    def step5(self):
        for group in range(len(self.groups)):
            self.made[group].wait_recv()
            own = self.gather(0, group)
            self.passed.append(
                self.batch(self.out.at[self.units(group), pl.ds(0, 512)])
            )
            self.passed[group].add(own, own, moved(self.here, c=1))

    def step6(self):
        for group, (order, _, _) in enumerate(self.groups):
            self.made[group].wait_recv()
            for step in (2, 1, 3):
                chunk = lax.rem(self.here[order[0]] + 4 - step, 4)
                piece = self.out.at[self.units(group), rows(self.base + chunk * 128, 128)]
                self.passed[group].add(piece, piece, moved(self.here, c=1))

    def step7(self, group):
        self.passed[group].wait_recv()

    def all7(self):
        for group in range(len(self.groups)):
            self.step7(group)


def sum_bufs(units, out=True):
    return [
        VMEM((units, 1024, 128), F32),
        VMEM((units, 512, 128), F32),
        VMEM((3, units, 128, 128), F32),
        VMEM((3, units, 32, 128), F32),
        VMEM((4, units, 32, 128), F32),
    ] + [VMEM((units, 1024, 128), F32)] * out


S_GROUPS = ((X, 0, 1), (Y, 1, 2), (Z, 3, 1))
Q_GROUPS = ((X, 0, 1), (Y, 1, 1), (Z, 2, 1))
E_GROUPS = (((X, 0, 2), (Y, 2, 1), (Z, 3, 1)), ((Z, 0, 2), (Y, 2, 1), (X, 3, 1)))

SHAPES = dict(
    series=((ROWS, LOOKBACK), BF16),
    w_embed=((LOOKBACK, WIDTH), BF16),
    w_query=((WIDTH, WIDTH), BF16),
    w_key=((WIDTH, WIDTH), BF16),
    w_value=((WIDTH, WIDTH), BF16),
    w_out=((WIDTH, WIDTH), BF16),
    proj=((KP, ROWS), BF16),
    cot=((ROWS, WIDTH), BF16),
    series_t=((LOOKBACK, ROWS), BF16),
    hid=((ROWS, WIDTH), BF16),
    hid_t=((WIDTH, ROWS), BF16),
    key_n=((PAIRS, KP, 128), F32),
    key_r=((PAIRS, KP, 128), F32),
    key_in=((PAIRS, 128, 512), BF16),
    key_out=((PAIRS, 512, 128), BF16),
    val_in=((PAIRS, 256, 512), BF16),
    val_out=((PAIRS, 512, 128), BF16),
    proj_t=((ROWS, KP), BF16),
    w_out_t=((WIDTH, WIDTH), BF16),
    w_query_t=((WIDTH, WIDTH), BF16),
    ph_core=((512, 128), F32),
    ph_plane=((15, 32, 128), F32),
    ph_x=((4, 32, 128), F32),
    ph=((1024, 128), F32),
)
LOADS = ("w_embed", "proj", "w_query", "cot", "w_out", "w_key", "w_value")
N_COPIES = 5 + 5 * 3 * 7


def layer_kernel(*refs):
    names = ("series", "w_embed", "w_query", "w_key", "w_value", "w_out", "proj", "cot")
    hbm = dict(zip(names, refs[:8]))
    out_hbm, embed_hbm, attn_hbm = refs[8:11]
    refs = refs[11:]
    v = dict(zip(SHAPES, refs[: len(SHAPES)]))
    for slot, name in enumerate(("att", "g_query", "g_hid", "out")):
        v[name] = v["series"].at[:, pl.ds(slot * WIDTH, WIDTH)]
    for slot, name in enumerate(("q_n", "g_att")):
        v[name] = v["w_embed"].at[pl.ds(slot * ROWS, ROWS)]
    refs = refs[len(SHAPES) :]
    s_bufs, q0_bufs, q1_bufs, e1_bufs = (refs[6 * i : 6 * i + 6] for i in range(4))
    e0_bufs = refs[24:29] + (s_bufs[0],)
    send, recv, load_sem, store_sem = refs[29:]
    v["q_r"] = e1_bufs[0]
    v["ph_in"] = e0_bufs[0].at[0]
    v["ph_half"] = e0_bufs[0].at[1, pl.ds(0, 512)]
    for side in range(2):
        where = pl.ds(side * KP, KP)
        v["gk", side] = v["hid_t"].at[where, pl.ds(0, WIDTH)]
        v["gv", side] = v["hid_t"].at[where, pl.ds(WIDTH, WIDTH)]
        v["back", side] = v["g_query"].at[where]
        v["ph_t", side] = v["g_hid"].at[pl.ds(0, WIDTH), pl.ds(side * KP, KP)]
    here = position()
    core, plane = here["c"], here["y"] * 4 + here["z"]
    base = core * 512

    def plane_device(step):
        there = lax.rem(plane + step, 16)
        return (here["x"] * 8 + lax.div(there, 4) * 2 + core, lax.rem(there, 4))

    loads = {}
    for slot, name in enumerate(LOADS):
        loads[name] = pltpu.make_async_copy(hbm[name], v[name], load_sem.at[slot])
    series_loads = []
    for block in range(BLOCKS):
        where = pl.ds(block * BLOCK, BLOCK)
        series_loads.append(
            pltpu.make_async_copy(
                hbm["series"].at[where], v["series"].at[where], load_sem.at[len(LOADS) + block]
            )
        )
    loads["w_embed"].start()
    for made in series_loads:
        made.start()
    loads["proj"].start()

    barrier = pltpu.get_barrier_semaphore()
    others = [moved(here, c=1)]
    others += [moved(here, x=step) for step in (1, 2, 3)]
    others += [plane_device(step) for step in range(1, 16)]
    for device in others:
        pl.semaphore_signal(barrier, inc=1, device_id=device, device_id_type=MESH)

    pool = Pool(send, recv)
    sum_s = Sum(here, pool, S_GROUPS, s_bufs)
    sum_q = [Sum(here, pool, Q_GROUPS, bufs) for bufs in (q0_bufs, q1_bufs)]
    sum_e = [Sum(here, pool, E_GROUPS[i], bufs) for i, bufs in enumerate((e0_bufs, e1_bufs))]

    lane = lax.broadcasted_iota(jnp.int32, (256, 128), 1) & 64
    row = lax.broadcasted_iota(jnp.int32, (256, 128), 0) & 64
    ones = jnp.where(lane == row, 1.0 / 64, 0.0).astype(BF16)

    def head_mean(values):
        return dot(jnp.concatenate(hi_lo(values), 1), ones)

    loads["w_embed"].wait()
    for block in range(BLOCKS):
        series_loads[block].wait()
        if block == 2:
            for name in LOADS[2:]:
                loads[name].start()
        where = pl.ds(block * BLOCK, BLOCK)
        v["hid"][where] = dot(v["series"][where], v["w_embed"][...]).astype(BF16)
    loads["proj"].wait()
    part = dot(v["proj"][...], v["hid"][...])
    for pair in range(PAIRS):
        v["ph_in"][pl.ds(pair * 256, 256)] = part[:, pair * 128 : pair * 128 + 128]

    pl.semaphore_wait(barrier, len(others))
    across = pool.batch(v["ph_core"])
    across.add(v["ph_in"].at[rows((1 - core) * 512, 512)], v["ph_core"], moved(here, c=1))

    loads["w_query"].wait()

    @pl.loop(0, BLOCKS)
    def _(block):
        where = rows(block * BLOCK, BLOCK)
        query = dot(v["hid"][where], v["w_query"][...])
        for pair in range(PAIRS):
            part = query[:, pair * 128 : pair * 128 + 128]
            factor = lax.rsqrt(head_mean(part * part) + 1e-06)
            v["q_r"][pair, where] = factor
            v["q_n"][where, pl.ds(pair * 128, 128)] = (part * factor).astype(BF16)

    across.wait_recv()
    v["ph_half"][...] = v["ph_in"][rows(base, 512)] + v["ph_core"][...]
    scattered = pool.batch(v["ph_plane"])
    for step in range(1, 16):
        there = lax.rem(plane + step, 16)
        scattered.add(
            v["ph_half"].at[rows(there * 32, 32)], v["ph_plane"].at[step - 1], plane_device(step)
        )

    @pl.loop(0, 8)
    def _(part):
        where = rows(part * 256, 256)
        v["series_t"][where] = v["series"][:, where].T

    own = pl.multiple_of(plane * 32, 32)
    v["proj_t"][...] = v["proj"][...].T
    @pl.loop(0, 8)
    def _(part):
        got = dot(v["series_t"][rows(part * 256, 256)], v["proj_t"][...])
        unit = lax.div(part, 4) * 2
        where = rows(lax.rem(part, 4) * 256, 256)
        sum_s.data[unit, where] = got[:, :128]
        sum_s.data[unit + 1, where] = got[:, 128:]

    scattered.wait_recv()
    total = v["ph_half"][pl.ds(own, 32)]
    for step in range(15):
        total = total + v["ph_plane"][step]
    v["ph_x"][here["x"]] = total
    mine = v["ph_x"].at[here["x"]]
    shares = pool.batch(v["ph_x"].at[pl.ds(0, 3)])
    for step in (2, 1, 3):
        shares.add(mine, mine, moved(here, x=step))
    for group in range(3):
        sum_s.core(group)

    loads["cot"].wait()
    loads["w_out"].wait()
    v["w_out_t"][...] = v["w_out"][...].T
    v["w_query_t"][...] = v["w_query"][...].T

    @pl.loop(0, BLOCKS)
    def _(block):
        where = rows(block * BLOCK, BLOCK)
        grad = dot(v["cot"][where], v["w_out_t"][...]).astype(BF16)
        v["g_att"][where] = grad

    shares.wait_recv()
    whole = (v["ph_x"][0] + v["ph_x"][1]) + (v["ph_x"][2] + v["ph_x"][3])
    mine = v["ph"].at[rows(base + own, 32)]
    mine[...] = whole
    spread = pool.batch(v["ph"].at[pl.ds(0, 480)])
    for step in range(1, 16):
        spread.add(mine, mine, plane_device(step))
    sum_s.step1()
    v["hid_t"][...] = v["hid"][...].T

    spread.wait_recv()
    mine = v["ph"].at[rows(base, 512)]
    passed = pool.batch(mine)
    passed.add(mine, mine, moved(here, c=1))
    passed.wait_recv()
    pool.drain([across, scattered])

    loads["w_key"].wait()
    loads["w_value"].wait()
    ph = jnp.concatenate([v["ph"][pl.ds(pair * 256, 256)] for pair in range(PAIRS)], 1)
    ph_hi, ph_lo = hi_lo(ph)
    low_half = lax.broadcasted_iota(jnp.int32, (256, 128), 1) < 64
    none = jnp.zeros((256, 128), BF16)
    keys = dot(ph_hi, v["w_key"][...]) + dot(ph_lo, v["w_key"][...])
    values = dot(ph_hi, v["w_value"][...]) + dot(ph_lo, v["w_value"][...])
    blank = jnp.zeros((64, 256), BF16)
    for pair in range(PAIRS):
        part = keys[:, pair * 128 : pair * 128 + 128]
        factor = lax.rsqrt(head_mean(part * part) + 1e-06)
        normed = part * factor
        v["key_n"][pair] = normed
        v["key_r"][pair] = factor
        eighth = (normed * 0.125).astype(BF16)
        v["key_out"][pair, :256] = jnp.where(low_half, eighth, none)
        v["key_out"][pair, 256:] = jnp.where(low_half, none, eighth)
        turned = eighth.T
        v["key_in"][pair, :64, :256] = turned[:64]
        v["key_in"][pair, 64:, 256:] = turned[64:]
        v["key_in"][pair, :64, 256:] = blank
        v["key_in"][pair, 64:, :256] = blank
        val_hi, val_lo = hi_lo(values[:, pair * 128 : pair * 128 + 128])
        v["val_out"][pair, :256] = jnp.where(low_half, val_hi, none)
        v["val_out"][pair, 256:] = jnp.where(low_half, none, val_hi)
        for index, value in enumerate((val_hi, val_lo)):
            turned = value.T
            at = index * 128
            v["val_in"][pair, at : at + 64, :256] = turned[:64]
            v["val_in"][pair, at + 64 : at + 128, 256:] = turned[64:]
            v["val_in"][pair, at : at + 64, 256:] = blank
            v["val_in"][pair, at + 64 : at + 128, :256] = blank

    def attention(pair):
        sums = sum_q[pair // 2].data
        first = (pair % 2) * 128
        lanes_of = pl.ds(pair * 128, 128)
        for part in range(4):
            sums[0, pl.ds(part * 256 + first, 128)] = jnp.zeros((128, 128), F32)

        @pl.loop(0, BLOCKS)
        def _(block):
            where = rows(block * BLOCK, BLOCK)
            query = v["q_n"][where, lanes_of]
            grad = v["g_att"][where, lanes_of]
            scores = dot(query, v["key_in"][pair])
            grad_probs = dot(jnp.concatenate([grad, grad], 1), v["val_in"][pair])
            query_t, grad_t = query.T, grad.T
            probs_b, grad_scores = [], []
            for head in range(2):
                lanes = slice(head * 256, head * 256 + 256)
                expo = jnp.exp(scores[:, lanes])
                probs = expo * (1.0 / jnp.sum(expo, axis=1, keepdims=True))
                grad_p = grad_probs[:, lanes]
                inner = jnp.sum(probs * grad_p, axis=1, keepdims=True)
                probs_b.append(probs.astype(BF16))
                grad_scores.append((probs * (grad_p - inner)).astype(BF16))
                for at, got in (
                    (0, dot(query_t[head * 64 : head * 64 + 64], grad_scores[head])),
                    (512, dot(grad_t[head * 64 : head * 64 + 64], probs_b[head])),
                ):
                    for side in range(2):
                        rest = pl.ds(at + side * 256 + first + head * 64, 64)
                        sums[0, rest] = sums[0, rest] + got[:, side * 128 : side * 128 + 128]
            attended = dot(jnp.concatenate(probs_b, 1), v["val_out"][pair])
            v["att"][where, lanes_of] = attended.astype(BF16)
            grad_n = dot(jnp.concatenate(grad_scores, 1), v["key_out"][pair])
            normed = query.astype(F32)
            grad_q = v["q_r"][pair, where] * (grad_n - normed * head_mean(grad_n * normed))
            v["g_query"][where, lanes_of] = grad_q.astype(BF16)

    def weight_grads(quad):
        both = pl.ds(quad * 256, 256)
        sums = sum_q[quad].data
        got = dot(v["att"][:, both].T, v["cot"][...])
        for part in range(4):
            sums[2, pl.ds(part * 256, 256)] = got[:, part * 128 : part * 128 + 128]
        sum_q[quad].core(0)
        got = dot(v["hid_t"][...], v["g_query"][:, both])
        for part in range(2):
            sums[1, pl.ds(part * 512, 512)] = got[:, part * 128 : part * 128 + 128]
        sum_q[quad].core(1)
        sum_q[quad].core(2)

    attention(0)
    sum_s.step2()
    attention(1)
    weight_grads(0)
    sum_s.step3()
    attention(2)
    sum_q[0].step1()
    sum_s.step4()
    attention(3)
    sum_q[0].step2()
    sum_s.step5()

    @pl.loop(0, BLOCKS)
    def _(block):
        where = rows(block * BLOCK, BLOCK)
        v["g_hid"][where] = (
            v["cot"][where].astype(F32) + dot(v["g_query"][where], v["w_query_t"][...])
        ).astype(BF16)

    weight_grads(1)
    sum_q[0].step3()

    def embed_part(index):
        @pl.loop(0, 4)
        def _(part):
            got = dot(v["series_t"][rows(index * 1024 + part * 256, 256)], v["g_hid"][...])
            where = rows(part * 256, 256)
            for unit in range(4):
                sum_e[index].data[unit, where] = got[:, unit * 128 : unit * 128 + 128]

        for group in range(3):
            sum_e[index].core(group)

    sum_s.settle()
    embed_part(0)
    sum_q[1].step1()
    embed_part(1)
    sum_e[0].step1()
    sum_q[0].step4()
    sum_s.step6()
    sum_e[1].step1()
    sum_q[1].step2()

    @pl.loop(0, BLOCKS)
    def _(block):
        where = rows(block * BLOCK, BLOCK)
        v["out"][where] = (
            v["hid"][where].astype(F32) + dot(v["att"][where], v["w_out"][...])
        ).astype(BF16)

    stores = []

    def store(src, dst):
        made = pltpu.make_async_copy(src, dst, store_sem.at[len(stores)])
        made.start()
        stores.append(made)

    store(v["out"], out_hbm)
    sum_e[0].step2()
    sum_q[0].step5()
    sum_q[1].step3()
    sum_e[1].step2()
    sum_e[0].step3()
    sum_q[1].step4()
    sum_q[0].step6()
    sum_e[1].step3()
    sum_e[0].step4()
    sum_q[1].step5()
    sum_e[1].step4()
    sum_e[0].step5()
    sum_q[0].all7()
    sum_s.all7()
    for side, part in enumerate(hi_lo(ph)):
        v["ph_t", side][...] = part.T
    sum_q[1].step6()
    sum_e[1].step5()
    sum_q[1].all7()
    for one in sum_e:
        one.settle()
    for one in sum_q:
        one.finish()

    for quad in range(2):
        for half in range(2):
            pair = quad * 2 + half
            lanes = pl.ds(pair * 128, 128)
            turned = []
            for at in (0, 512):
                turned.append(
                    jnp.concatenate(
                        [
                            sum_q[quad].out[0, pl.ds(at + side * 256 + half * 128, 128)]
                            for side in range(2)
                        ],
                        1,
                    ).T
                )
            grad_n = turned[0] * 0.125
            normed = v["key_n"][pair]
            grad_k = v["key_r"][pair] * (grad_n - normed * head_mean(grad_n * normed))
            for index, (name, value) in enumerate((("gk", grad_k), ("gv", turned[1]))):
                for side, part in enumerate(hi_lo(value)):
                    v[name, side][:, lanes] = part
    back = dot_t(v["gk", 0][...], v["w_key"][...]) + dot_t(v["gk", 1][...], v["w_key"][...])
    back = back + dot_t(v["gv", 0][...], v["w_value"][...]) + dot_t(v["gv", 1][...], v["w_value"][...])
    for side, part in enumerate(hi_lo(back)):
        v["back", side][...] = part
    for index, name in enumerate(("gk", "gv")):
        got = dot(v["ph_t", 0][...], v[name, 0][...]) + dot(v["ph_t", 0][...], v[name, 1][...])
        got = (got + dot(v["ph_t", 1][...], v[name, 0][...])) * NORM
        for part in range(4):
            where = (part // 2, pl.ds((part % 2) * 512, 512))
            sum_q[index].data[where] = got[:, part * 128 : part * 128 + 128]
            store(sum_q[index].data.at[where], attn_hbm.at[1 + index, :, pl.ds(part * 128, 128)])
    for quad in range(2):
        out = sum_q[quad].out

        @pl.loop(1, 3)
        def _(unit):
            out[unit] = out[unit] * NORM

        for part in range(2):
            store(
                out.at[1, pl.ds(part * 512, 512)],
                attn_hbm.at[0, :, pl.ds(quad * 256 + part * 128, 128)],
            )
        for part in range(4):
            store(
                out.at[2, pl.ds(part * 256, 256)],
                attn_hbm.at[3, pl.ds(quad * 256, 256), pl.ds(part * 128, 128)],
            )
    sum_e[0].step6()
    sum_e[1].step6()
    for index in range(2):

        @pl.loop(0, 4)
        def _(part):
            where = rows(part * 256, 256)
            left = jnp.concatenate([sum_s.out[index * 2 + side, where] for side in range(2)], 1)
            left_hi, left_lo = hi_lo(left)
            got = dot(left_hi, v["back", 0][...]) + dot(left_hi, v["back", 1][...])
            got = got + dot(left_lo, v["back", 0][...])
            for unit in range(4):
                sum_e[index].data[unit, where] = got[:, unit * 128 : unit * 128 + 128]

    for index in range(2):
        for group, (_, start, size) in enumerate(E_GROUPS[index]):
            sum_e[index].step7(group)
        sum_e[index].finish()
        for unit in range(4):

            @pl.loop(0, 4)
            def _(part):
                where = (unit, rows(part * 256, 256))
                sum_e[index].out[where] = (
                    sum_e[index].out[where] + sum_e[index].data[where]
                ) * NORM

            store(
                sum_e[index].out.at[unit],
                embed_hbm.at[pl.ds(index * 1024, 1024), pl.ds(unit * 128, 128)],
            )
    pool.drain()
    for made in stores:
        made.wait()


def local(series, w_embed, w_query, w_key, w_value, w_out, proj, cotangent):
    anywhere = pl.BlockSpec(memory_space=pl.ANY)
    return pl.pallas_call(
        layer_kernel,
        out_shape=(
            jax.ShapeDtypeStruct((ROWS, WIDTH), BF16),
            jax.ShapeDtypeStruct((LOOKBACK, WIDTH), F32),
            jax.ShapeDtypeStruct((4, WIDTH, WIDTH), F32),
        ),
        in_specs=[anywhere] * 8,
        out_specs=(anywhere,) * 3,
        scratch_shapes=[VMEM(shape, dtype) for shape, dtype in SHAPES.values()]
        + sum_bufs(4)
        + sum_bufs(3) * 2
        + sum_bufs(4)
        + sum_bufs(4, False)
        + [
            pltpu.SemaphoreType.DMA((N_COPIES,)),
            pltpu.SemaphoreType.DMA((N_COPIES,)),
            pltpu.SemaphoreType.DMA((len(LOADS) + BLOCKS,)),
            pltpu.SemaphoreType.DMA((32,)),
        ],
        compiler_params=pltpu.CompilerParams(
            collective_id=0, has_side_effects=True, vmem_limit_bytes=63 * 1024 * 1024
        ),
    )(series, w_embed, w_query, w_key, w_value, w_out, proj, cotangent)


def solution(mesh):
    return jax.shard_map(
        local,
        mesh=mesh,
        in_specs=(
            P(("var", "grp"), None),
            P(),
            P(),
            P(),
            P(),
            P(),
            P(None, ("var", "grp")),
            P(("var", "grp"), None),
        ),
        out_specs=(P(("var", "grp"), None), P(), P()),
        check_vma=False,
    )
```

```python
import functools
import math

import jax
import jax.numpy as jnp
from jax import lax
from jax.experimental import pallas as pl
from jax.experimental.pallas import tpu as pltpu
from jax.sharding import PartitionSpec as P

MESH = pl.DeviceIdType.MESH
F32 = jnp.float32
BF16 = jnp.bfloat16
VMEM = pltpu.VMEM
ROWS = 1024
WIDTH = 512
LOOKBACK = 2048
KP = 256
PAIRS = 4
BLOCK = 512
LOADS_OF_SERIES = 4
BLOCKS = ROWS // BLOCK
NORM = 1.0 / math.sqrt(131072.0)


def dot(left, right, dims=((1,), (0,))):
    return lax.dot_general(left, right, (dims, ((), ())), preferred_element_type=F32)


def dot_t(left, right):
    return dot(left, right, ((1,), (1,)))


def hi_lo(values):
    upper = values.astype(BF16)
    return upper, (values - upper.astype(F32)).astype(BF16)


def rows(start, size, step=None):
    return pl.ds(pl.multiple_of(start, step or size), size)


def position():
    var = lax.axis_index("var")
    return {
        "x": lax.div(var, 8),
        "y": lax.rem(lax.div(var, 2), 4),
        "c": lax.rem(var, 2),
        "z": lax.axis_index("grp"),
    }


def moved(place, **steps):
    there = dict(place)
    for axis, step in steps.items():
        there[axis] = lax.rem(place[axis] + step, 2 if axis == "c" else 4)
    return (there["x"] * 8 + there["y"] * 2 + there["c"], there["z"])


class Batch:
    def __init__(self, pool, whole):
        slot = pool.count
        pool.count += 1
        pool.open.append(self)
        self.send, self.recv, self.whole = pool.send.at[slot], pool.recv.at[slot], whole

    def add(self, src, dst, device):
        self.device = device
        self.copy(src, dst).start()

    def copy(self, src, dst):
        return pltpu.make_async_remote_copy(
            src_ref=src,
            dst_ref=dst,
            send_sem=self.send,
            recv_sem=self.recv,
            device_id=self.device,
            device_id_type=MESH,
        )

    def wait_recv(self):
        self.copy(self.whole, self.whole).wait_recv()

    def wait_send(self):
        self.copy(self.whole, self.whole).wait_send()


class Pool:
    def __init__(self, send, recv):
        self.send, self.recv, self.count, self.open = send, recv, 0, []

    def batch(self, whole):
        return Batch(self, whole)

    def drain(self, batches=None):
        for one in list(self.open) if batches is None else batches:
            one.wait_send()
            self.open.remove(one)


X, Y, Z = ("x", "y", "z"), ("y", "z", "x"), ("z", "x", "y")


class Sum:
    def __init__(self, here, pool, groups, bufs):
        self.here, self.pool, self.groups = here, pool, groups
        self.data, self.half, self.one, self.two, self.three, self.out = bufs
        self.base = here["c"] * 512
        self.across = []
        self.made = {}
        self.passed = []
        self.sends = []
        self.batches = []

    def batch(self, whole):
        self.batches.append(self.pool.batch(whole))
        return self.batches[-1]

    def finish(self):
        self.pool.drain([one for one in self.batches if one in self.pool.open])

    def units(self, group):
        return pl.ds(self.groups[group][1], self.groups[group][2])

    def core(self, group):
        units = self.units(group)
        self.across.append(self.batch(self.half.at[units]))
        self.sends.append(self.across[-1])
        self.across[-1].add(
            self.data.at[units, rows((1 - self.here["c"]) * 512, 512)],
            self.half.at[units],
            moved(self.here, c=1),
        )

    def place(self, group, level):
        at = self.base
        for axis, size in zip(self.groups[group][0][:level], (128, 32)):
            at = at + self.here[axis] * size
        return at

    def scatter(self, level, group):
        units = self.units(group)
        axis = self.groups[group][0][level]
        extent = (128, 32)[level]
        buffer = (self.one, self.two)[level]
        at = self.place(group, level)
        self.made[group] = self.batch(buffer.at[:, units])
        self.sends.append(self.made[group])
        for step in (2, 1, 3):
            self.made[group].add(
                self.data.at[
                    units, rows(at + lax.rem(self.here[axis] + step, 4) * extent, extent)
                ],
                buffer.at[step - 1, units],
                moved(self.here, **{axis: step}),
            )

    def settle(self):
        self.pool.drain(self.sends)

    def gather(self, level, group):
        units = self.units(group)
        axis = self.groups[group][0][level]
        extent = (128, 32)[level]
        own = self.out.at[units, rows(self.place(group, level + 1), extent)]
        self.made[group] = self.batch(self.out.at[units, pl.ds(0, 3 * extent)])
        for step in (2, 1, 3):
            self.made[group].add(own, own, moved(self.here, **{axis: step}))
        return own

    def step1(self):
        for group, (_, start, size) in enumerate(self.groups):
            self.across[group].wait_recv()

            @pl.loop(start, start + size)
            def _(unit):
                where = (unit, rows(self.base, 512))
                self.data[where] = self.data[where] + self.half[unit]

            self.scatter(0, group)

    def reduced(self, level, group):
        order = self.groups[group][0]
        extent = (128, 32)[level]
        buffer = (self.one, self.two)[level]
        self.made[group].wait_recv()
        units = self.units(group)
        where = (units, rows(self.place(group, level + 1), extent))
        total = (self.data[where] + buffer[0, units]) + (buffer[1, units] + buffer[2, units])
        if level == 0:
            self.data[where] = total
        else:
            mine = (self.here[order[2]], units)
            self.three[mine] = total
            self.made[group] = self.batch(self.three.at[pl.ds(0, 3), units])
            for step in (2, 1, 3):
                self.made[group].add(
                    self.three.at[mine],
                    self.three.at[mine],
                    moved(self.here, **{order[2]: step}),
                )

    def step2(self):
        for group in range(len(self.groups)):
            self.reduced(0, group)
            self.scatter(1, group)

    def step3(self):
        for group in range(len(self.groups)):
            self.reduced(1, group)

    def step4(self):
        for group in range(len(self.groups)):
            self.made[group].wait_recv()
            units = self.units(group)
            part = [self.three[index, units] for index in range(4)]
            where = (units, rows(self.place(group, 2), 32))
            self.out[where] = (part[0] + part[1]) + (part[2] + part[3])
            self.gather(1, group)

    def step5(self):
        for group in range(len(self.groups)):
            self.made[group].wait_recv()
            own = self.gather(0, group)
            self.passed.append(
                self.batch(self.out.at[self.units(group), pl.ds(0, 512)])
            )
            self.passed[group].add(own, own, moved(self.here, c=1))

    def step6(self):
        for group, (order, _, _) in enumerate(self.groups):
            self.made[group].wait_recv()
            for step in (2, 1, 3):
                chunk = lax.rem(self.here[order[0]] + 4 - step, 4)
                piece = self.out.at[self.units(group), rows(self.base + chunk * 128, 128)]
                self.passed[group].add(piece, piece, moved(self.here, c=1))

    def step7(self, group):
        self.passed[group].wait_recv()

    def all7(self):
        for group in range(len(self.groups)):
            self.step7(group)


def sum_bufs(units, out=True):
    return [
        VMEM((units, 1024, 128), F32),
        VMEM((units, 512, 128), F32),
        VMEM((3, units, 128, 128), F32),
        VMEM((3, units, 32, 128), F32),
        VMEM((4, units, 32, 128), F32),
    ] + [VMEM((units, 1024, 128), F32)] * out


S_GROUPS = ((X, 0, 1), (Y, 1, 2), (Z, 3, 1))
Q_GROUPS = ((X, 0, 1), (Y, 1, 1), (Z, 2, 1))
E_GROUPS = (((X, 0, 2), (Y, 2, 1), (Z, 3, 1)), ((Z, 0, 2), (Y, 2, 1), (X, 3, 1)))

SHAPES = dict(
    series=((ROWS, LOOKBACK), BF16),
    w_embed=((LOOKBACK, WIDTH), BF16),
    w_query=((WIDTH, WIDTH), BF16),
    w_key=((WIDTH, WIDTH), BF16),
    w_value=((WIDTH, WIDTH), BF16),
    w_out=((WIDTH, WIDTH), BF16),
    proj=((KP, ROWS), BF16),
    cot=((ROWS, WIDTH), BF16),
    series_t=((LOOKBACK, ROWS), BF16),
    hid=((ROWS, WIDTH), BF16),
    hid_t=((WIDTH, ROWS), BF16),
    key_n=((PAIRS, KP, 128), F32),
    key_r=((PAIRS, KP, 128), F32),
    key_in=((PAIRS, 128, 512), BF16),
    key_out=((PAIRS, 512, 128), BF16),
    val_in=((PAIRS, 256, 512), BF16),
    val_out=((PAIRS, 512, 128), BF16),
    proj_t=((ROWS, KP), BF16),
    w_out_t=((WIDTH, WIDTH), BF16),
    w_query_t=((WIDTH, WIDTH), BF16),
    ph_core=((512, 128), F32),
    ph_plane=((15, 32, 128), F32),
    ph_x=((4, 32, 128), F32),
    ph=((1024, 128), F32),
)
LOADS = ("w_embed", "proj", "w_query", "cot", "w_out", "w_key", "w_value")
N_COPIES = 5 + 5 * 3 * 7


def layer_kernel(*refs):
    names = ("series", "w_embed", "w_query", "w_key", "w_value", "w_out", "proj", "cot")
    hbm = dict(zip(names, refs[:8]))
    out_hbm, embed_hbm, attn_hbm = refs[8:11]
    refs = refs[11:]
    v = dict(zip(SHAPES, refs[: len(SHAPES)]))
    for slot, name in enumerate(("att", "g_query", "g_hid", "out")):
        v[name] = v["series"].at[:, pl.ds(slot * WIDTH, WIDTH)]
    for slot, name in enumerate(("q_n", "g_att")):
        v[name] = v["w_embed"].at[pl.ds(slot * ROWS, ROWS)]
    refs = refs[len(SHAPES) :]
    s_bufs, q0_bufs, q1_bufs, e1_bufs = (refs[6 * i : 6 * i + 6] for i in range(4))
    e0_bufs = refs[24:29] + (s_bufs[0],)
    send, recv, load_sem, store_sem = refs[29:]
    v["q_r"] = e1_bufs[0]
    v["ph_in"] = e0_bufs[0].at[0]
    v["ph_half"] = e0_bufs[0].at[1, pl.ds(0, 512)]
    for side in range(2):
        where = pl.ds(side * KP, KP)
        v["gk", side] = v["hid_t"].at[where, pl.ds(0, WIDTH)]
        v["gv", side] = v["hid_t"].at[where, pl.ds(WIDTH, WIDTH)]
        v["back", side] = v["g_query"].at[where]
        v["ph_t", side] = v["g_hid"].at[pl.ds(0, WIDTH), pl.ds(side * KP, KP)]
    here = position()
    core, plane = here["c"], here["y"] * 4 + here["z"]
    base = core * 512

    def plane_device(step):
        there = lax.rem(plane + step, 16)
        return (here["x"] * 8 + lax.div(there, 4) * 2 + core, lax.rem(there, 4))

    loads = {}
    for slot, name in enumerate(LOADS):
        loads[name] = pltpu.make_async_copy(hbm[name], v[name], load_sem.at[slot])
    series_loads = []
    for block in range(LOADS_OF_SERIES):
        where = pl.ds(block * 256, 256)
        series_loads.append(
            pltpu.make_async_copy(
                hbm["series"].at[where], v["series"].at[where], load_sem.at[len(LOADS) + block]
            )
        )
    loads["w_embed"].start()
    for made in series_loads:
        made.start()
    loads["proj"].start()

    barrier = pltpu.get_barrier_semaphore()
    others = [moved(here, c=1)]
    others += [moved(here, x=step) for step in (1, 2, 3)]
    others += [plane_device(step) for step in range(1, 16)]
    for device in others:
        pl.semaphore_signal(barrier, inc=1, device_id=device, device_id_type=MESH)

    pool = Pool(send, recv)
    sum_s = Sum(here, pool, S_GROUPS, s_bufs)
    sum_q = [Sum(here, pool, Q_GROUPS, bufs) for bufs in (q0_bufs, q1_bufs)]
    sum_e = [Sum(here, pool, E_GROUPS[i], bufs) for i, bufs in enumerate((e0_bufs, e1_bufs))]

    lane = lax.broadcasted_iota(jnp.int32, (256, 128), 1) & 64
    row = lax.broadcasted_iota(jnp.int32, (256, 128), 0) & 64
    ones = jnp.where(lane == row, 1.0 / 64, 0.0).astype(BF16)

    def head_mean(values):
        return dot(jnp.concatenate(hi_lo(values), 1), ones)

    loads["w_embed"].wait()
    for block in range(BLOCKS):
        series_loads[2 * block].wait()
        series_loads[2 * block + 1].wait()
        if block == 1:
            for name in LOADS[2:]:
                loads[name].start()
        where = pl.ds(block * BLOCK, BLOCK)
        v["hid"][where] = dot(v["series"][where], v["w_embed"][...]).astype(BF16)
    loads["proj"].wait()
    part = dot(v["proj"][...], v["hid"][...])
    for pair in range(PAIRS):
        v["ph_in"][pl.ds(pair * 256, 256)] = part[:, pair * 128 : pair * 128 + 128]

    pl.semaphore_wait(barrier, len(others))
    across = pool.batch(v["ph_core"])
    across.add(v["ph_in"].at[rows((1 - core) * 512, 512)], v["ph_core"], moved(here, c=1))

    loads["w_query"].wait()

    @pl.loop(0, BLOCKS)
    def _(block):
        where = rows(block * BLOCK, BLOCK)
        query = dot(v["hid"][where], v["w_query"][...])
        for pair in range(PAIRS):
            part = query[:, pair * 128 : pair * 128 + 128]
            factor = lax.rsqrt(head_mean(part * part) + 1e-06)
            v["q_r"][pair, where] = factor
            v["q_n"][where, pl.ds(pair * 128, 128)] = (part * factor).astype(BF16)

    across.wait_recv()
    v["ph_half"][...] = v["ph_in"][rows(base, 512)] + v["ph_core"][...]
    scattered = pool.batch(v["ph_plane"])
    for step in range(1, 16):
        there = lax.rem(plane + step, 16)
        scattered.add(
            v["ph_half"].at[rows(there * 32, 32)], v["ph_plane"].at[step - 1], plane_device(step)
        )

    @pl.loop(0, 8)
    def _(part):
        where = rows(part * 256, 256)
        v["series_t"][where] = v["series"][:, where].T

    own = pl.multiple_of(plane * 32, 32)
    v["proj_t"][...] = v["proj"][...].T
    @pl.loop(0, 4)
    def _(part):
        got = dot(v["series_t"][rows(part * 512, 512)], v["proj_t"][...])
        unit = lax.div(part, 2) * 2
        where = rows(lax.rem(part, 2) * 512, 512)
        sum_s.data[unit, where] = got[:, :128]
        sum_s.data[unit + 1, where] = got[:, 128:]

    scattered.wait_recv()
    total = v["ph_half"][pl.ds(own, 32)]
    for step in range(15):
        total = total + v["ph_plane"][step]
    v["ph_x"][here["x"]] = total
    mine = v["ph_x"].at[here["x"]]
    shares = pool.batch(v["ph_x"].at[pl.ds(0, 3)])
    for step in (2, 1, 3):
        shares.add(mine, mine, moved(here, x=step))
    for group in range(3):
        sum_s.core(group)

    loads["cot"].wait()
    loads["w_out"].wait()
    v["w_out_t"][...] = v["w_out"][...].T
    v["w_query_t"][...] = v["w_query"][...].T

    @pl.loop(0, BLOCKS)
    def _(block):
        where = rows(block * BLOCK, BLOCK)
        grad = dot(v["cot"][where], v["w_out_t"][...]).astype(BF16)
        v["g_att"][where] = grad

    shares.wait_recv()
    whole = (v["ph_x"][0] + v["ph_x"][1]) + (v["ph_x"][2] + v["ph_x"][3])
    mine = v["ph"].at[rows(base + own, 32)]
    mine[...] = whole
    spread = pool.batch(v["ph"].at[pl.ds(0, 480)])
    for step in range(1, 16):
        spread.add(mine, mine, plane_device(step))
    sum_s.step1()
    v["hid_t"][...] = v["hid"][...].T

    spread.wait_recv()
    mine = v["ph"].at[rows(base, 512)]
    passed = pool.batch(mine)
    passed.add(mine, mine, moved(here, c=1))
    passed.wait_recv()
    pool.drain([across, scattered])
    sum_s.step2()

    loads["w_key"].wait()
    loads["w_value"].wait()
    ph = jnp.concatenate([v["ph"][pl.ds(pair * 256, 256)] for pair in range(PAIRS)], 1)
    ph_hi, ph_lo = hi_lo(ph)
    low_half = lax.broadcasted_iota(jnp.int32, (256, 128), 1) < 64
    none = jnp.zeros((256, 128), BF16)
    keys = dot(ph_hi, v["w_key"][...]) + dot(ph_lo, v["w_key"][...])
    values = dot(ph_hi, v["w_value"][...]) + dot(ph_lo, v["w_value"][...])
    blank = jnp.zeros((64, 256), BF16)
    for pair in range(PAIRS):
        part = keys[:, pair * 128 : pair * 128 + 128]
        factor = lax.rsqrt(head_mean(part * part) + 1e-06)
        normed = part * factor
        v["key_n"][pair] = normed
        v["key_r"][pair] = factor
        eighth = (normed * 0.125).astype(BF16)
        v["key_out"][pair, :256] = jnp.where(low_half, eighth, none)
        v["key_out"][pair, 256:] = jnp.where(low_half, none, eighth)
        turned = eighth.T
        v["key_in"][pair, :64, :256] = turned[:64]
        v["key_in"][pair, 64:, 256:] = turned[64:]
        v["key_in"][pair, :64, 256:] = blank
        v["key_in"][pair, 64:, :256] = blank
        val_hi, val_lo = hi_lo(values[:, pair * 128 : pair * 128 + 128])
        v["val_out"][pair, :256] = jnp.where(low_half, val_hi, none)
        v["val_out"][pair, 256:] = jnp.where(low_half, none, val_hi)
        for index, value in enumerate((val_hi, val_lo)):
            turned = value.T
            at = index * 128
            v["val_in"][pair, at : at + 64, :256] = turned[:64]
            v["val_in"][pair, at + 64 : at + 128, 256:] = turned[64:]
            v["val_in"][pair, at : at + 64, 256:] = blank
            v["val_in"][pair, at + 64 : at + 128, :256] = blank

    def attention(pair):
        sums = sum_q[pair // 2].data
        first = (pair % 2) * 128
        lanes_of = pl.ds(pair * 128, 128)
        for part in range(4):
            sums[0, pl.ds(part * 256 + first, 128)] = jnp.zeros((128, 128), F32)

        @pl.loop(0, BLOCKS)
        def _(block):
            where = rows(block * BLOCK, BLOCK)
            query = v["q_n"][where, lanes_of]
            grad = v["g_att"][where, lanes_of]
            scores = dot(query, v["key_in"][pair])
            grad_probs = dot(jnp.concatenate([grad, grad], 1), v["val_in"][pair])
            query_t, grad_t = query.T, grad.T
            probs_b, grad_scores = [], []
            for head in range(2):
                lanes = slice(head * 256, head * 256 + 256)
                expo = jnp.exp(scores[:, lanes])
                probs = expo * (1.0 / jnp.sum(expo, axis=1, keepdims=True))
                grad_p = grad_probs[:, lanes]
                inner = jnp.sum(probs * grad_p, axis=1, keepdims=True)
                probs_b.append(probs.astype(BF16))
                grad_scores.append((probs * (grad_p - inner)).astype(BF16))
                for at, got in (
                    (0, dot(query_t[head * 64 : head * 64 + 64], grad_scores[head])),
                    (512, dot(grad_t[head * 64 : head * 64 + 64], probs_b[head])),
                ):
                    for side in range(2):
                        rest = pl.ds(at + side * 256 + first + head * 64, 64)
                        sums[0, rest] = sums[0, rest] + got[:, side * 128 : side * 128 + 128]
            attended = dot(jnp.concatenate(probs_b, 1), v["val_out"][pair])
            v["att"][where, lanes_of] = attended.astype(BF16)
            grad_n = dot(jnp.concatenate(grad_scores, 1), v["key_out"][pair])
            normed = query.astype(F32)
            grad_q = v["q_r"][pair, where] * (grad_n - normed * head_mean(grad_n * normed))
            v["g_query"][where, lanes_of] = grad_q.astype(BF16)

    def weight_grads(quad):
        both = pl.ds(quad * 256, 256)
        sums = sum_q[quad].data
        got = dot(v["att"][:, both].T, v["cot"][...])
        for part in range(4):
            sums[2, pl.ds(part * 256, 256)] = got[:, part * 128 : part * 128 + 128]
        sum_q[quad].core(0)
        got = dot(v["hid_t"][...], v["g_query"][:, both])
        for part in range(2):
            sums[1, pl.ds(part * 512, 512)] = got[:, part * 128 : part * 128 + 128]
        sum_q[quad].core(1)
        sum_q[quad].core(2)

    attention(0)
    attention(1)
    weight_grads(0)
    sum_s.step3()
    attention(2)
    attention(3)
    sum_q[0].step1()
    sum_s.step4()

    @pl.loop(0, BLOCKS)
    def _(block):
        where = rows(block * BLOCK, BLOCK)
        v["g_hid"][where] = (
            v["cot"][where].astype(F32) + dot(v["g_query"][where], v["w_query_t"][...])
        ).astype(BF16)

    weight_grads(1)

    def embed_part(index):
        @pl.loop(0, 2)
        def _(part):
            got = dot(v["series_t"][rows(index * 1024 + part * 512, 512)], v["g_hid"][...])
            where = rows(part * 512, 512)
            for unit in range(4):
                sum_e[index].data[unit, where] = got[:, unit * 128 : unit * 128 + 128]

        for group in range(3):
            sum_e[index].core(group)

    sum_s.settle()
    embed_part(0)
    sum_q[1].step1()
    sum_q[0].step2()
    embed_part(1)
    sum_e[0].step1()
    sum_s.step5()
    sum_e[1].step1()
    sum_q[1].step2()
    sum_q[0].step3()

    @pl.loop(0, BLOCKS)
    def _(block):
        where = rows(block * BLOCK, BLOCK)
        v["out"][where] = (
            v["hid"][where].astype(F32) + dot(v["att"][where], v["w_out"][...])
        ).astype(BF16)

    stores = []

    def store(src, dst):
        made = pltpu.make_async_copy(src, dst, store_sem.at[len(stores)])
        made.start()
        stores.append(made)

    store(v["out"], out_hbm)
    sum_e[0].step2()
    sum_q[1].step3()
    sum_q[0].step4()
    sum_e[1].step2()
    sum_e[0].step3()
    sum_q[1].step4()
    sum_s.step6()
    sum_q[0].step5()
    sum_e[1].step3()
    sum_e[0].step4()
    sum_q[1].step5()
    sum_e[1].step4()
    sum_e[0].step5()
    sum_q[0].step6()
    sum_s.all7()
    sum_q[0].all7()
    for side, part in enumerate(hi_lo(ph)):
        v["ph_t", side][...] = part.T
    sum_q[1].step6()
    sum_e[1].step5()
    sum_q[1].all7()
    for one in sum_e:
        one.settle()
    for one in sum_q:
        one.finish()

    for quad in range(2):
        for half in range(2):
            pair = quad * 2 + half
            lanes = pl.ds(pair * 128, 128)
            turned = []
            for at in (0, 512):
                turned.append(
                    jnp.concatenate(
                        [
                            sum_q[quad].out[0, pl.ds(at + side * 256 + half * 128, 128)]
                            for side in range(2)
                        ],
                        1,
                    ).T
                )
            grad_n = turned[0] * 0.125
            normed = v["key_n"][pair]
            grad_k = v["key_r"][pair] * (grad_n - normed * head_mean(grad_n * normed))
            for index, (name, value) in enumerate((("gk", grad_k), ("gv", turned[1]))):
                for side, part in enumerate(hi_lo(value)):
                    v[name, side][:, lanes] = part
    back = dot_t(v["gk", 0][...], v["w_key"][...]) + dot_t(v["gk", 1][...], v["w_key"][...])
    back = back + dot_t(v["gv", 0][...], v["w_value"][...]) + dot_t(v["gv", 1][...], v["w_value"][...])
    for side, part in enumerate(hi_lo(back)):
        v["back", side][...] = part
    for index, name in enumerate(("gk", "gv")):
        got = dot(v["ph_t", 0][...], v[name, 0][...]) + dot(v["ph_t", 0][...], v[name, 1][...])
        got = (got + dot(v["ph_t", 1][...], v[name, 0][...])) * NORM
        for part in range(4):
            where = (part // 2, pl.ds((part % 2) * 512, 512))
            sum_q[index].data[where] = got[:, part * 128 : part * 128 + 128]
            store(sum_q[index].data.at[where], attn_hbm.at[1 + index, :, pl.ds(part * 128, 128)])
    for quad in range(2):
        out = sum_q[quad].out

        @pl.loop(1, 3)
        def _(unit):
            out[unit] = out[unit] * NORM

        for part in range(2):
            store(
                out.at[1, pl.ds(part * 512, 512)],
                attn_hbm.at[0, :, pl.ds(quad * 256 + part * 128, 128)],
            )
        for part in range(4):
            store(
                out.at[2, pl.ds(part * 256, 256)],
                attn_hbm.at[3, pl.ds(quad * 256, 256), pl.ds(part * 128, 128)],
            )
    sum_e[0].step6()
    sum_e[1].step6()
    for index in range(2):

        @pl.loop(0, 4)
        def _(part):
            where = rows(part * 256, 256)
            left = jnp.concatenate([sum_s.out[index * 2 + side, where] for side in range(2)], 1)
            left_hi, left_lo = hi_lo(left)
            got = dot(left_hi, v["back", 0][...]) + dot(left_hi, v["back", 1][...])
            got = got + dot(left_lo, v["back", 0][...])
            for unit in range(4):
                sum_e[index].data[unit, where] = got[:, unit * 128 : unit * 128 + 128]

    for index in range(2):
        for group, (_, start, size) in enumerate(E_GROUPS[index]):
            sum_e[index].step7(group)
        sum_e[index].finish()
        for unit in range(4):

            @pl.loop(0, 4)
            def _(part):
                where = (unit, rows(part * 256, 256))
                sum_e[index].out[where] = (
                    sum_e[index].out[where] + sum_e[index].data[where]
                ) * NORM

            store(
                sum_e[index].out.at[unit],
                embed_hbm.at[pl.ds(index * 1024, 1024), pl.ds(unit * 128, 128)],
            )
    pool.drain()
    for made in stores:
        made.wait()


def local(series, w_embed, w_query, w_key, w_value, w_out, proj, cotangent):
    anywhere = pl.BlockSpec(memory_space=pl.ANY)
    return pl.pallas_call(
        layer_kernel,
        out_shape=(
            jax.ShapeDtypeStruct((ROWS, WIDTH), BF16),
            jax.ShapeDtypeStruct((LOOKBACK, WIDTH), F32),
            jax.ShapeDtypeStruct((4, WIDTH, WIDTH), F32),
        ),
        in_specs=[anywhere] * 8,
        out_specs=(anywhere,) * 3,
        scratch_shapes=[VMEM(shape, dtype) for shape, dtype in SHAPES.values()]
        + sum_bufs(4)
        + sum_bufs(3) * 2
        + sum_bufs(4)
        + sum_bufs(4, False)
        + [
            pltpu.SemaphoreType.DMA((N_COPIES,)),
            pltpu.SemaphoreType.DMA((N_COPIES,)),
            pltpu.SemaphoreType.DMA((len(LOADS) + LOADS_OF_SERIES,)),
            pltpu.SemaphoreType.DMA((32,)),
        ],
        compiler_params=pltpu.CompilerParams(
            collective_id=0, has_side_effects=True, vmem_limit_bytes=63 * 1024 * 1024
        ),
    )(series, w_embed, w_query, w_key, w_value, w_out, proj, cotangent)


def solution(mesh):
    return jax.shard_map(
        local,
        mesh=mesh,
        in_specs=(
            P(("var", "grp"), None),
            P(),
            P(),
            P(),
            P(),
            P(),
            P(None, ("var", "grp")),
            P(("var", "grp"), None),
        ),
        out_specs=(P(("var", "grp"), None), P(), P()),
        check_vma=False,
    )
```

```python
import functools
import math

import jax
import jax.numpy as jnp
from jax import lax
from jax.experimental import pallas as pl
from jax.experimental.pallas import tpu as pltpu
from jax.sharding import PartitionSpec as P

MESH = pl.DeviceIdType.MESH
F32 = jnp.float32
BF16 = jnp.bfloat16
VMEM = pltpu.VMEM
ROWS = 1024
WIDTH = 512
LOOKBACK = 2048
KP = 256
PAIRS = 4
BLOCK = 512
ATTENTION_BLOCK = 512
LOADS_OF_SERIES = 4
BLOCKS = ROWS // BLOCK
NORM = 1.0 / math.sqrt(131072.0)


def dot(left, right, dims=((1,), (0,))):
    return lax.dot_general(left, right, (dims, ((), ())), preferred_element_type=F32)


def dot_t(left, right):
    return dot(left, right, ((1,), (1,)))


def hi_lo(values):
    upper = values.astype(BF16)
    return upper, (values - upper.astype(F32)).astype(BF16)


def rows(start, size, step=None):
    return pl.ds(pl.multiple_of(start, step or size), size)


def position():
    var = lax.axis_index("var")
    return {
        "x": lax.div(var, 8),
        "y": lax.rem(lax.div(var, 2), 4),
        "c": lax.rem(var, 2),
        "z": lax.axis_index("grp"),
    }


def moved(place, **steps):
    there = dict(place)
    for axis, step in steps.items():
        there[axis] = lax.rem(place[axis] + step, 2 if axis == "c" else 4)
    return (there["x"] * 8 + there["y"] * 2 + there["c"], there["z"])


class Batch:
    def __init__(self, pool, whole):
        slot = pool.count
        pool.count += 1
        pool.open.append(self)
        self.send, self.recv, self.whole = pool.send.at[slot], pool.recv.at[slot], whole
        self.arrived = False

    def add(self, src, dst, device):
        self.device = device
        self.copy(src, dst).start()

    def copy(self, src, dst):
        return pltpu.make_async_remote_copy(
            src_ref=src,
            dst_ref=dst,
            send_sem=self.send,
            recv_sem=self.recv,
            device_id=self.device,
            device_id_type=MESH,
        )

    def wait_recv(self):
        if not self.arrived:
            self.copy(self.whole, self.whole).wait_recv()
        self.arrived = True

    def wait_send(self):
        self.copy(self.whole, self.whole).wait_send()


class Pool:
    def __init__(self, send, recv):
        self.send, self.recv, self.count, self.open = send, recv, 0, []

    def batch(self, whole):
        return Batch(self, whole)

    def drain(self, batches=None):
        for one in list(self.open) if batches is None else batches:
            one.wait_send()
            self.open.remove(one)


X, Y, Z = ("x", "y", "z"), ("y", "z", "x"), ("z", "x", "y")


class Sum:
    def __init__(self, here, pool, groups, bufs, joined=False):
        self.joined = joined
        self.here, self.pool, self.groups = here, pool, groups
        self.data, self.half, self.one, self.two, self.three, self.out = bufs
        self.base = here["c"] * 512
        self.across = []
        self.made = {}
        self.passed = []
        self.sends = []
        self.batches = []

    def batch(self, group, whole, first):
        if self.joined and group > 0:
            return first
        self.batches.append(self.pool.batch(whole(self.waits(group))))
        return self.batches[-1]

    def waits(self, group):
        return slice(None) if self.joined else self.units(group)

    def finish(self):
        self.pool.drain([one for one in self.batches if one in self.pool.open])

    def units(self, group):
        return pl.ds(self.groups[group][1], self.groups[group][2])

    def core(self, group):
        units = self.units(group)
        first = self.across[0] if self.across else None
        self.across.append(self.batch(group, lambda some: self.half.at[some], first))
        self.sends.append(self.across[-1])
        self.across[-1].add(
            self.data.at[units, rows((1 - self.here["c"]) * 512, 512)],
            self.half.at[units],
            moved(self.here, c=1),
        )

    def place(self, group, level):
        at = self.base
        for axis, size in zip(self.groups[group][0][:level], (128, 32)):
            at = at + self.here[axis] * size
        return at

    def scatter(self, level, group):
        units = self.units(group)
        axis = self.groups[group][0][level]
        extent = (128, 32)[level]
        buffer = (self.one, self.two)[level]
        at = self.place(group, level)
        self.made[group] = self.batch(group, lambda some: buffer.at[:, some], self.made.get(0))
        self.sends.append(self.made[group])
        for step in (2, 1, 3):
            self.made[group].add(
                self.data.at[
                    units, rows(at + lax.rem(self.here[axis] + step, 4) * extent, extent)
                ],
                buffer.at[step - 1, units],
                moved(self.here, **{axis: step}),
            )

    def settle(self):
        self.pool.drain([one for one in self.batches if one in self.sends])

    def gather(self, level, group):
        units = self.units(group)
        axis = self.groups[group][0][level]
        extent = (128, 32)[level]
        own = self.out.at[units, rows(self.place(group, level + 1), extent)]
        self.made[group] = self.batch(
            group, lambda some: self.out.at[some, pl.ds(0, 3 * extent)], self.made.get(0)
        )
        for step in (2, 1, 3):
            self.made[group].add(own, own, moved(self.here, **{axis: step}))
        return own

    def step1(self):
        for group, (_, start, size) in enumerate(self.groups):
            self.across[group].wait_recv()

            @pl.loop(start, start + size)
            def _(unit):
                where = (unit, rows(self.base, 512))
                self.data[where] = self.data[where] + self.half[unit]

            self.scatter(0, group)

    def reduced(self, level, group):
        order = self.groups[group][0]
        extent = (128, 32)[level]
        buffer = (self.one, self.two)[level]
        self.made[group].wait_recv()
        units = self.units(group)
        where = (units, rows(self.place(group, level + 1), extent))
        total = (self.data[where] + buffer[0, units]) + (buffer[1, units] + buffer[2, units])
        if level == 0:
            self.data[where] = total
        else:
            mine = (self.here[order[2]], units)
            self.three[mine] = total
            self.made[group] = self.batch(
                group, lambda some: self.three.at[pl.ds(0, 3), some], self.made.get(0)
            )
            for step in (2, 1, 3):
                self.made[group].add(
                    self.three.at[mine],
                    self.three.at[mine],
                    moved(self.here, **{order[2]: step}),
                )

    def step2(self):
        for group in range(len(self.groups)):
            self.reduced(0, group)
            self.scatter(1, group)

    def step3(self):
        for group in range(len(self.groups)):
            self.reduced(1, group)

    def step4(self):
        for group in range(len(self.groups)):
            self.made[group].wait_recv()
            units = self.units(group)
            part = [self.three[index, units] for index in range(4)]
            where = (units, rows(self.place(group, 2), 32))
            self.out[where] = (part[0] + part[1]) + (part[2] + part[3])
            self.gather(1, group)

    def step5(self):
        for group in range(len(self.groups)):
            self.made[group].wait_recv()
            own = self.gather(0, group)
            first = self.passed[0] if self.passed else None
            self.passed.append(
                self.batch(group, lambda some: self.out.at[some, pl.ds(0, 512)], first)
            )
            self.passed[group].add(own, own, moved(self.here, c=1))

    def step6(self):
        for group, (order, _, _) in enumerate(self.groups):
            self.made[group].wait_recv()
            for step in (2, 1, 3):
                chunk = lax.rem(self.here[order[0]] + 4 - step, 4)
                piece = self.out.at[self.units(group), rows(self.base + chunk * 128, 128)]
                self.passed[group].add(piece, piece, moved(self.here, c=1))

    def step7(self, group):
        self.passed[group].wait_recv()

    def all7(self):
        for group in range(len(self.groups)):
            self.step7(group)


def sum_bufs(units, out=True):
    return [
        VMEM((units, 1024, 128), F32),
        VMEM((units, 512, 128), F32),
        VMEM((3, units, 128, 128), F32),
        VMEM((3, units, 32, 128), F32),
        VMEM((4, units, 32, 128), F32),
    ] + [VMEM((units, 1024, 128), F32)] * out


S_GROUPS = ((X, 0, 1), (Y, 1, 2), (Z, 3, 1))
Q_GROUPS = ((X, 0, 1), (Y, 1, 1), (Z, 2, 1))
E_GROUPS = (((X, 0, 2), (Y, 2, 1), (Z, 3, 1)), ((Z, 0, 2), (Y, 2, 1), (X, 3, 1)))

SHAPES = dict(
    series=((ROWS, LOOKBACK), BF16),
    w_embed=((LOOKBACK, WIDTH), BF16),
    w_query=((WIDTH, WIDTH), BF16),
    w_key=((WIDTH, WIDTH), BF16),
    w_value=((WIDTH, WIDTH), BF16),
    w_out=((WIDTH, WIDTH), BF16),
    proj=((KP, ROWS), BF16),
    cot=((ROWS, WIDTH), BF16),
    series_t=((LOOKBACK, ROWS), BF16),
    hid=((ROWS, WIDTH), BF16),
    hid_t=((WIDTH, ROWS), BF16),
    key_n=((PAIRS, KP, 128), F32),
    key_r=((PAIRS, KP, 128), F32),
    key_in=((PAIRS, 128, 512), BF16),
    key_out=((PAIRS, 512, 128), BF16),
    val_in=((PAIRS, 256, 512), BF16),
    val_out=((PAIRS, 512, 128), BF16),
    proj_t=((ROWS, KP), BF16),
    w_out_t=((WIDTH, WIDTH), BF16),
    w_query_t=((WIDTH, WIDTH), BF16),
    ph_core=((512, 128), F32),
    ph_plane=((15, 32, 128), F32),
    ph_x=((4, 32, 128), F32),
    ph=((1024, 128), F32),
)
LOADS = ("w_embed", "proj", "w_query", "cot", "w_out", "w_key", "w_value")
N_COPIES = 5 + 3 * 7 + 2 * 3 * 7


def layer_kernel(*refs):
    names = ("series", "w_embed", "w_query", "w_key", "w_value", "w_out", "proj", "cot")
    hbm = dict(zip(names, refs[:8]))
    out_hbm, embed_hbm, attn_hbm = refs[8:11]
    refs = refs[11:]
    v = dict(zip(SHAPES, refs[: len(SHAPES)]))
    for slot, name in enumerate(("att", "g_query", "g_hid", "out")):
        v[name] = v["series"].at[:, pl.ds(slot * WIDTH, WIDTH)]
    for slot, name in enumerate(("q_n", "g_att")):
        v[name] = v["w_embed"].at[pl.ds(slot * ROWS, ROWS)]
    refs = refs[len(SHAPES) :]
    s_bufs, q0_bufs, q1_bufs, e1_bufs = (refs[6 * i : 6 * i + 6] for i in range(4))
    e0_bufs = refs[24:29] + (s_bufs[0],)
    send, recv, load_sem, store_sem = refs[29:]
    v["q_r"] = e1_bufs[0]
    v["ph_in"] = e0_bufs[0].at[0]
    v["ph_half"] = e0_bufs[0].at[1, pl.ds(0, 512)]
    for side in range(2):
        where = pl.ds(side * KP, KP)
        v["gk", side] = v["hid_t"].at[where, pl.ds(0, WIDTH)]
        v["gv", side] = v["hid_t"].at[where, pl.ds(WIDTH, WIDTH)]
        v["back", side] = v["g_query"].at[where]
        v["ph_t", side] = v["g_hid"].at[pl.ds(0, WIDTH), pl.ds(side * KP, KP)]
    here = position()
    core, plane = here["c"], here["y"] * 4 + here["z"]
    base = core * 512

    def plane_device(step):
        there = lax.rem(plane + step, 16)
        return (here["x"] * 8 + lax.div(there, 4) * 2 + core, lax.rem(there, 4))

    loads = {}
    for slot, name in enumerate(LOADS):
        loads[name] = pltpu.make_async_copy(hbm[name], v[name], load_sem.at[slot])
    series_loads = []
    for block in range(LOADS_OF_SERIES):
        where = pl.ds(block * 256, 256)
        series_loads.append(
            pltpu.make_async_copy(
                hbm["series"].at[where], v["series"].at[where], load_sem.at[len(LOADS) + block]
            )
        )
    loads["w_embed"].start()
    for made in series_loads:
        made.start()
    loads["proj"].start()

    barrier = pltpu.get_barrier_semaphore()
    others = [moved(here, c=1)]
    others += [moved(here, x=step) for step in (1, 2, 3)]
    others += [plane_device(step) for step in range(1, 16)]
    for device in others:
        pl.semaphore_signal(barrier, inc=1, device_id=device, device_id_type=MESH)

    pool = Pool(send, recv)
    sum_s = Sum(here, pool, S_GROUPS, s_bufs, True)
    sum_q = [Sum(here, pool, Q_GROUPS, bufs, True) for bufs in (q0_bufs, q1_bufs)]
    sum_e = [Sum(here, pool, E_GROUPS[i], bufs) for i, bufs in enumerate((e0_bufs, e1_bufs))]

    lane = lax.broadcasted_iota(jnp.int32, (256, 128), 1) & 64
    row = lax.broadcasted_iota(jnp.int32, (256, 128), 0) & 64
    ones = jnp.where(lane == row, 1.0 / 64, 0.0).astype(BF16)

    def head_mean(values):
        return dot(jnp.concatenate(hi_lo(values), 1), ones)

    loads["w_embed"].wait()
    for block in range(BLOCKS):
        series_loads[2 * block].wait()
        series_loads[2 * block + 1].wait()
        if block == 1:
            for name in LOADS[2:]:
                loads[name].start()
        where = pl.ds(block * BLOCK, BLOCK)
        v["hid"][where] = dot(v["series"][where], v["w_embed"][...]).astype(BF16)
    loads["proj"].wait()
    part = dot(v["proj"][...], v["hid"][...])
    for pair in range(PAIRS):
        v["ph_in"][pl.ds(pair * 256, 256)] = part[:, pair * 128 : pair * 128 + 128]

    pl.semaphore_wait(barrier, len(others))
    across = pool.batch(v["ph_core"])
    across.add(v["ph_in"].at[rows((1 - core) * 512, 512)], v["ph_core"], moved(here, c=1))

    across.wait_recv()
    v["ph_half"][...] = v["ph_in"][rows(base, 512)] + v["ph_core"][...]
    scattered = pool.batch(v["ph_plane"])
    for step in range(1, 16):
        there = lax.rem(plane + step, 16)
        scattered.add(
            v["ph_half"].at[rows(there * 32, 32)], v["ph_plane"].at[step - 1], plane_device(step)
        )

    @pl.loop(0, 8)
    def _(part):
        where = rows(part * 256, 256)
        v["series_t"][where] = v["series"][:, where].T

    loads["w_query"].wait()

    @pl.loop(0, BLOCKS)
    def _(block):
        where = rows(block * BLOCK, BLOCK)
        query = dot(v["hid"][where], v["w_query"][...])
        for pair in range(PAIRS):
            part = query[:, pair * 128 : pair * 128 + 128]
            factor = lax.rsqrt(head_mean(part * part) + 1e-06)
            v["q_r"][pair, where] = factor
            v["q_n"][where, pl.ds(pair * 128, 128)] = (part * factor).astype(BF16)

    own = pl.multiple_of(plane * 32, 32)
    v["proj_t"][...] = v["proj"][...].T
    @pl.loop(0, 4)
    def _(part):
        got = dot(v["series_t"][rows(part * 512, 512)], v["proj_t"][...])
        unit = lax.div(part, 2) * 2
        where = rows(lax.rem(part, 2) * 512, 512)
        sum_s.data[unit, where] = got[:, :128]
        sum_s.data[unit + 1, where] = got[:, 128:]

    scattered.wait_recv()
    total = v["ph_half"][pl.ds(own, 32)]
    for step in range(15):
        total = total + v["ph_plane"][step]
    v["ph_x"][here["x"]] = total
    mine = v["ph_x"].at[here["x"]]
    shares = pool.batch(v["ph_x"].at[pl.ds(0, 3)])
    for step in (2, 1, 3):
        shares.add(mine, mine, moved(here, x=step))
    for group in range(3):
        sum_s.core(group)

    loads["cot"].wait()
    loads["w_out"].wait()
    v["w_out_t"][...] = v["w_out"][...].T
    v["w_query_t"][...] = v["w_query"][...].T

    @pl.loop(0, BLOCKS)
    def _(block):
        where = rows(block * BLOCK, BLOCK)
        grad = dot(v["cot"][where], v["w_out_t"][...]).astype(BF16)
        v["g_att"][where] = grad

    shares.wait_recv()
    whole = (v["ph_x"][0] + v["ph_x"][1]) + (v["ph_x"][2] + v["ph_x"][3])
    mine = v["ph"].at[rows(base + own, 32)]
    mine[...] = whole
    spread = pool.batch(v["ph"].at[pl.ds(0, 480)])
    for step in range(1, 16):
        spread.add(mine, mine, plane_device(step))
    sum_s.step1()
    v["hid_t"][...] = v["hid"][...].T

    spread.wait_recv()
    mine = v["ph"].at[rows(base, 512)]
    passed = pool.batch(mine)
    passed.add(mine, mine, moved(here, c=1))
    passed.wait_recv()
    pool.drain([across, scattered])
    sum_s.step2()

    loads["w_key"].wait()
    loads["w_value"].wait()
    ph = jnp.concatenate([v["ph"][pl.ds(pair * 256, 256)] for pair in range(PAIRS)], 1)
    ph_hi, ph_lo = hi_lo(ph)
    low_half = lax.broadcasted_iota(jnp.int32, (256, 128), 1) < 64
    none = jnp.zeros((256, 128), BF16)
    keys = dot(ph_hi, v["w_key"][...]) + dot(ph_lo, v["w_key"][...])
    values = dot(ph_hi, v["w_value"][...]) + dot(ph_lo, v["w_value"][...])
    blank = jnp.zeros((64, 256), BF16)
    for pair in range(PAIRS):
        part = keys[:, pair * 128 : pair * 128 + 128]
        factor = lax.rsqrt(head_mean(part * part) + 1e-06)
        normed = part * factor
        v["key_n"][pair] = normed
        v["key_r"][pair] = factor
        eighth = (normed * 0.125).astype(BF16)
        v["key_out"][pair, :256] = jnp.where(low_half, eighth, none)
        v["key_out"][pair, 256:] = jnp.where(low_half, none, eighth)
        turned = eighth.T
        v["key_in"][pair, :64, :256] = turned[:64]
        v["key_in"][pair, 64:, 256:] = turned[64:]
        v["key_in"][pair, :64, 256:] = blank
        v["key_in"][pair, 64:, :256] = blank
        val_hi, val_lo = hi_lo(values[:, pair * 128 : pair * 128 + 128])
        v["val_out"][pair, :256] = jnp.where(low_half, val_hi, none)
        v["val_out"][pair, 256:] = jnp.where(low_half, none, val_hi)
        for index, value in enumerate((val_hi, val_lo)):
            turned = value.T
            at = index * 128
            v["val_in"][pair, at : at + 64, :256] = turned[:64]
            v["val_in"][pair, at + 64 : at + 128, 256:] = turned[64:]
            v["val_in"][pair, at : at + 64, 256:] = blank
            v["val_in"][pair, at + 64 : at + 128, :256] = blank

    def attention(pair):
        sums = sum_q[pair // 2].data
        first = (pair % 2) * 128
        lanes_of = pl.ds(pair * 128, 128)
        for part in range(4):
            sums[0, pl.ds(part * 256 + first, 128)] = jnp.zeros((128, 128), F32)

        @pl.loop(0, ROWS // ATTENTION_BLOCK, unroll=2)
        def _(block):
            where = rows(block * ATTENTION_BLOCK, ATTENTION_BLOCK)
            query = v["q_n"][where, lanes_of]
            grad = v["g_att"][where, lanes_of]
            scores = dot(query, v["key_in"][pair])
            grad_probs = dot(jnp.concatenate([grad, grad], 1), v["val_in"][pair])
            query_t, grad_t = query.T, grad.T
            probs_b, grad_scores = [], []
            for head in range(2):
                lanes = slice(head * 256, head * 256 + 256)
                expo = jnp.exp(scores[:, lanes])
                probs = expo * (1.0 / jnp.sum(expo, axis=1, keepdims=True))
                grad_p = grad_probs[:, lanes]
                inner = jnp.sum(probs * grad_p, axis=1, keepdims=True)
                probs_b.append(probs.astype(BF16))
                grad_scores.append((probs * (grad_p - inner)).astype(BF16))
                for at, got in (
                    (0, dot(query_t[head * 64 : head * 64 + 64], grad_scores[head])),
                    (512, dot(grad_t[head * 64 : head * 64 + 64], probs_b[head])),
                ):
                    for side in range(2):
                        rest = pl.ds(at + side * 256 + first + head * 64, 64)
                        sums[0, rest] = sums[0, rest] + got[:, side * 128 : side * 128 + 128]
            attended = dot(jnp.concatenate(probs_b, 1), v["val_out"][pair])
            v["att"][where, lanes_of] = attended.astype(BF16)
            grad_n = dot(jnp.concatenate(grad_scores, 1), v["key_out"][pair])
            normed = query.astype(F32)
            grad_q = v["q_r"][pair, where] * (grad_n - normed * head_mean(grad_n * normed))
            v["g_query"][where, lanes_of] = grad_q.astype(BF16)

    def weight_grads(quad):
        both = pl.ds(quad * 256, 256)
        sums = sum_q[quad].data
        got = dot(v["att"][:, both].T, v["cot"][...])
        for part in range(4):
            sums[2, pl.ds(part * 256, 256)] = got[:, part * 128 : part * 128 + 128]
        sum_q[quad].core(0)
        got = dot(v["hid_t"][...], v["g_query"][:, both])
        for part in range(2):
            sums[1, pl.ds(part * 512, 512)] = got[:, part * 128 : part * 128 + 128]
        sum_q[quad].core(1)
        sum_q[quad].core(2)

    attention(0)
    attention(1)
    weight_grads(0)
    sum_s.step3()
    attention(2)
    attention(3)
    sum_q[0].step1()
    sum_s.step4()

    @pl.loop(0, BLOCKS)
    def _(block):
        where = rows(block * BLOCK, BLOCK)
        v["g_hid"][where] = (
            v["cot"][where].astype(F32) + dot(v["g_query"][where], v["w_query_t"][...])
        ).astype(BF16)

    weight_grads(1)

    def embed_part(index):
        @pl.loop(0, 2)
        def _(part):
            got = dot(v["series_t"][rows(index * 1024 + part * 512, 512)], v["g_hid"][...])
            where = rows(part * 512, 512)
            for unit in range(4):
                sum_e[index].data[unit, where] = got[:, unit * 128 : unit * 128 + 128]

        for group in range(3):
            sum_e[index].core(group)

    sum_s.settle()
    embed_part(0)
    sum_q[1].step1()
    sum_q[0].step2()
    embed_part(1)
    sum_e[0].step1()
    sum_s.step5()
    sum_e[1].step1()
    sum_q[1].step2()
    sum_q[0].step3()

    @pl.loop(0, BLOCKS)
    def _(block):
        where = rows(block * BLOCK, BLOCK)
        v["out"][where] = (
            v["hid"][where].astype(F32) + dot(v["att"][where], v["w_out"][...])
        ).astype(BF16)

    stores = []

    def store(src, dst):
        made = pltpu.make_async_copy(src, dst, store_sem.at[len(stores)])
        made.start()
        stores.append(made)

    store(v["out"], out_hbm)
    sum_e[0].step2()
    sum_q[1].step3()
    sum_q[0].step4()
    sum_e[1].step2()
    sum_e[0].step3()
    sum_q[1].step4()
    sum_s.step6()
    sum_q[0].step5()
    sum_e[1].step3()
    sum_e[0].step4()
    sum_q[1].step5()
    sum_e[1].step4()
    sum_e[0].step5()
    sum_q[0].step6()
    sum_s.all7()
    sum_q[0].all7()
    for side, part in enumerate(hi_lo(ph)):
        v["ph_t", side][...] = part.T
    sum_q[1].step6()
    sum_e[1].step5()
    sum_q[1].all7()
    for one in sum_e:
        one.settle()
    for one in sum_q:
        one.finish()

    for quad in range(2):
        for half in range(2):
            pair = quad * 2 + half
            lanes = pl.ds(pair * 128, 128)
            turned = []
            for at in (0, 512):
                turned.append(
                    jnp.concatenate(
                        [
                            sum_q[quad].out[0, pl.ds(at + side * 256 + half * 128, 128)]
                            for side in range(2)
                        ],
                        1,
                    ).T
                )
            grad_n = turned[0] * 0.125
            normed = v["key_n"][pair]
            grad_k = v["key_r"][pair] * (grad_n - normed * head_mean(grad_n * normed))
            for index, (name, value) in enumerate((("gk", grad_k), ("gv", turned[1]))):
                for side, part in enumerate(hi_lo(value)):
                    v[name, side][:, lanes] = part
    back = dot_t(v["gk", 0][...], v["w_key"][...]) + dot_t(v["gk", 1][...], v["w_key"][...])
    back = back + dot_t(v["gv", 0][...], v["w_value"][...]) + dot_t(v["gv", 1][...], v["w_value"][...])
    for side, part in enumerate(hi_lo(back)):
        v["back", side][...] = part
    for index, name in enumerate(("gk", "gv")):
        got = dot(v["ph_t", 0][...], v[name, 0][...]) + dot(v["ph_t", 0][...], v[name, 1][...])
        got = (got + dot(v["ph_t", 1][...], v[name, 0][...])) * NORM
        for part in range(4):
            where = (part // 2, pl.ds((part % 2) * 512, 512))
            sum_q[index].data[where] = got[:, part * 128 : part * 128 + 128]
            store(sum_q[index].data.at[where], attn_hbm.at[1 + index, :, pl.ds(part * 128, 128)])
    for quad in range(2):
        out = sum_q[quad].out

        @pl.loop(1, 3)
        def _(unit):
            out[unit] = out[unit] * NORM

        for part in range(2):
            store(
                out.at[1, pl.ds(part * 512, 512)],
                attn_hbm.at[0, :, pl.ds(quad * 256 + part * 128, 128)],
            )
        for part in range(4):
            store(
                out.at[2, pl.ds(part * 256, 256)],
                attn_hbm.at[3, pl.ds(quad * 256, 256), pl.ds(part * 128, 128)],
            )
    sum_e[0].step6()
    sum_e[1].step6()
    for index in range(2):

        @pl.loop(0, 4)
        def _(part):
            where = rows(part * 256, 256)
            left = jnp.concatenate([sum_s.out[index * 2 + side, where] for side in range(2)], 1)
            left_hi, left_lo = hi_lo(left)
            got = dot(left_hi, v["back", 0][...]) + dot(left_hi, v["back", 1][...])
            got = got + dot(left_lo, v["back", 0][...])
            for unit in range(4):
                sum_e[index].data[unit, where] = got[:, unit * 128 : unit * 128 + 128]

    for index in range(2):
        for group, (_, start, size) in enumerate(E_GROUPS[index]):
            sum_e[index].step7(group)
        sum_e[index].finish()
        for unit in range(4):

            @pl.loop(0, 4)
            def _(part):
                where = (unit, rows(part * 256, 256))
                sum_e[index].out[where] = (
                    sum_e[index].out[where] + sum_e[index].data[where]
                ) * NORM

            store(
                sum_e[index].out.at[unit],
                embed_hbm.at[pl.ds(index * 1024, 1024), pl.ds(unit * 128, 128)],
            )
    pool.drain()
    for made in stores:
        made.wait()


def local(series, w_embed, w_query, w_key, w_value, w_out, proj, cotangent):
    anywhere = pl.BlockSpec(memory_space=pl.ANY)
    return pl.pallas_call(
        layer_kernel,
        out_shape=(
            jax.ShapeDtypeStruct((ROWS, WIDTH), BF16),
            jax.ShapeDtypeStruct((LOOKBACK, WIDTH), F32),
            jax.ShapeDtypeStruct((4, WIDTH, WIDTH), F32),
        ),
        in_specs=[anywhere] * 8,
        out_specs=(anywhere,) * 3,
        scratch_shapes=[VMEM(shape, dtype) for shape, dtype in SHAPES.values()]
        + sum_bufs(4)
        + sum_bufs(3) * 2
        + sum_bufs(4)
        + sum_bufs(4, False)
        + [
            pltpu.SemaphoreType.DMA((N_COPIES,)),
            pltpu.SemaphoreType.DMA((N_COPIES,)),
            pltpu.SemaphoreType.DMA((len(LOADS) + LOADS_OF_SERIES,)),
            pltpu.SemaphoreType.DMA((32,)),
        ],
        compiler_params=pltpu.CompilerParams(
            collective_id=0, has_side_effects=True, vmem_limit_bytes=63 * 1024 * 1024
        ),
    )(series, w_embed, w_query, w_key, w_value, w_out, proj, cotangent)


def solution(mesh):
    return jax.shard_map(
        local,
        mesh=mesh,
        in_specs=(
            P(("var", "grp"), None),
            P(),
            P(),
            P(),
            P(),
            P(),
            P(None, ("var", "grp")),
            P(("var", "grp"), None),
        ),
        out_specs=(P(("var", "grp"), None), P(), P()),
        check_vma=False,
    )
```

```python
import functools
import math

import jax
import jax.numpy as jnp
from jax import lax
from jax.experimental import pallas as pl
from jax.experimental.pallas import tpu as pltpu
from jax.sharding import PartitionSpec as P

MESH = pl.DeviceIdType.MESH
F32 = jnp.float32
BF16 = jnp.bfloat16
VMEM = pltpu.VMEM
ROWS = 1024
WIDTH = 512
LOOKBACK = 2048
KP = 256
PAIRS = 4
BLOCK = 512
ATTENTION_BLOCK = 512
LOADS_OF_SERIES = 4
BLOCKS = ROWS // BLOCK
NORM = 1.0 / math.sqrt(131072.0)


def dot(left, right, dims=((1,), (0,))):
    return lax.dot_general(left, right, (dims, ((), ())), preferred_element_type=F32)


def dot_t(left, right):
    return dot(left, right, ((1,), (1,)))


def hi_lo(values):
    upper = values.astype(BF16)
    return upper, (values - upper.astype(F32)).astype(BF16)


def rows(start, size, step=None):
    return pl.ds(pl.multiple_of(start, step or size), size)


def position():
    var = lax.axis_index("var")
    return {
        "x": lax.div(var, 8),
        "y": lax.rem(lax.div(var, 2), 4),
        "c": lax.rem(var, 2),
        "z": lax.axis_index("grp"),
    }


def moved(place, **steps):
    there = dict(place)
    for axis, step in steps.items():
        there[axis] = lax.rem(place[axis] + step, 2 if axis == "c" else 4)
    return (there["x"] * 8 + there["y"] * 2 + there["c"], there["z"])


class Batch:
    def __init__(self, pool, whole):
        slot = pool.count
        pool.count += 1
        pool.open.append(self)
        self.send, self.recv, self.whole = pool.send.at[slot], pool.recv.at[slot], whole
        self.arrived = False

    def add(self, src, dst, device):
        self.device = device
        self.copy(src, dst).start()

    def copy(self, src, dst):
        return pltpu.make_async_remote_copy(
            src_ref=src,
            dst_ref=dst,
            send_sem=self.send,
            recv_sem=self.recv,
            device_id=self.device,
            device_id_type=MESH,
        )

    def wait_recv(self):
        if not self.arrived:
            self.copy(self.whole, self.whole).wait_recv()
        self.arrived = True

    def wait_send(self):
        self.copy(self.whole, self.whole).wait_send()


class Pool:
    def __init__(self, send, recv):
        self.send, self.recv, self.count, self.open = send, recv, 0, []

    def batch(self, whole):
        return Batch(self, whole)

    def drain(self, batches=None):
        for one in list(self.open) if batches is None else batches:
            one.wait_send()
            self.open.remove(one)


X, Y, Z = ("x", "y", "z"), ("y", "z", "x"), ("z", "x", "y")


class Sum:
    def __init__(self, here, pool, groups, bufs, joined=False):
        self.joined = joined
        self.here, self.pool, self.groups = here, pool, groups
        self.data, self.half, self.one, self.two, self.three, self.out = bufs
        self.base = here["c"] * 512
        self.across = []
        self.made = {}
        self.passed = []
        self.sends = []
        self.batches = []

    def batch(self, group, whole, first):
        if self.joined and group > 0:
            return first
        self.batches.append(self.pool.batch(whole(self.waits(group))))
        return self.batches[-1]

    def waits(self, group):
        return slice(None) if self.joined else self.units(group)

    def finish(self):
        self.pool.drain([one for one in self.batches if one in self.pool.open])

    def units(self, group):
        return pl.ds(self.groups[group][1], self.groups[group][2])

    def core(self, group):
        units = self.units(group)
        first = self.across[0] if self.across else None
        self.across.append(self.batch(group, lambda some: self.half.at[some], first))
        self.sends.append(self.across[-1])
        self.across[-1].add(
            self.data.at[units, rows((1 - self.here["c"]) * 512, 512)],
            self.half.at[units],
            moved(self.here, c=1),
        )

    def place(self, group, level):
        at = self.base
        for axis, size in zip(self.groups[group][0][:level], (128, 32)):
            at = at + self.here[axis] * size
        return at

    def scatter(self, level, group):
        units = self.units(group)
        axis = self.groups[group][0][level]
        extent = (128, 32)[level]
        buffer = (self.one, self.two)[level]
        at = self.place(group, level)
        self.made[group] = self.batch(group, lambda some: buffer.at[:, some], self.made.get(0))
        self.sends.append(self.made[group])
        for step in (2, 1, 3):
            self.made[group].add(
                self.data.at[
                    units, rows(at + lax.rem(self.here[axis] + step, 4) * extent, extent)
                ],
                buffer.at[step - 1, units],
                moved(self.here, **{axis: step}),
            )

    def settle(self):
        self.pool.drain([one for one in self.batches if one in self.sends])

    def gather(self, level, group):
        units = self.units(group)
        axis = self.groups[group][0][level]
        extent = (128, 32)[level]
        own = self.out.at[units, rows(self.place(group, level + 1), extent)]
        self.made[group] = self.batch(
            group, lambda some: self.out.at[some, pl.ds(0, 3 * extent)], self.made.get(0)
        )
        for step in (2, 1, 3):
            self.made[group].add(own, own, moved(self.here, **{axis: step}))
        return own

    def step1(self):
        for group, (_, start, size) in enumerate(self.groups):
            self.across[group].wait_recv()

            @pl.loop(start, start + size)
            def _(unit):
                where = (unit, rows(self.base, 512))
                self.data[where] = self.data[where] + self.half[unit]

            self.scatter(0, group)

    def reduced(self, level, group):
        order = self.groups[group][0]
        extent = (128, 32)[level]
        buffer = (self.one, self.two)[level]
        self.made[group].wait_recv()
        units = self.units(group)
        where = (units, rows(self.place(group, level + 1), extent))
        total = (self.data[where] + buffer[0, units]) + (buffer[1, units] + buffer[2, units])
        if level == 0:
            self.data[where] = total
        else:
            mine = (self.here[order[2]], units)
            self.three[mine] = total
            self.made[group] = self.batch(
                group, lambda some: self.three.at[pl.ds(0, 3), some], self.made.get(0)
            )
            for step in (2, 1, 3):
                self.made[group].add(
                    self.three.at[mine],
                    self.three.at[mine],
                    moved(self.here, **{order[2]: step}),
                )

    def step2(self):
        for group in range(len(self.groups)):
            self.reduced(0, group)
            self.scatter(1, group)

    def step3(self):
        for group in range(len(self.groups)):
            self.reduced(1, group)

    def step4(self):
        for group in range(len(self.groups)):
            self.made[group].wait_recv()
            units = self.units(group)
            part = [self.three[index, units] for index in range(4)]
            where = (units, rows(self.place(group, 2), 32))
            self.out[where] = (part[0] + part[1]) + (part[2] + part[3])
            self.gather(1, group)

    def step5(self):
        for group in range(len(self.groups)):
            self.made[group].wait_recv()
            own = self.gather(0, group)
            first = self.passed[0] if self.passed else None
            self.passed.append(
                self.batch(group, lambda some: self.out.at[some, pl.ds(0, 512)], first)
            )
            self.passed[group].add(own, own, moved(self.here, c=1))

    def step6(self):
        for group, (order, _, _) in enumerate(self.groups):
            self.made[group].wait_recv()
            for step in (2, 1, 3):
                chunk = lax.rem(self.here[order[0]] + 4 - step, 4)
                piece = self.out.at[self.units(group), rows(self.base + chunk * 128, 128)]
                self.passed[group].add(piece, piece, moved(self.here, c=1))

    def step7(self, group):
        self.passed[group].wait_recv()

    def all7(self):
        for group in range(len(self.groups)):
            self.step7(group)


def sum_bufs(units, out=True):
    return [
        VMEM((units, 1024, 128), F32),
        VMEM((units, 512, 128), F32),
        VMEM((3, units, 128, 128), F32),
        VMEM((3, units, 32, 128), F32),
        VMEM((4, units, 32, 128), F32),
    ] + [VMEM((units, 1024, 128), F32)] * out


S_GROUPS = ((X, 0, 1), (Y, 1, 2), (Z, 3, 1))
Q_GROUPS = ((X, 0, 1), (Y, 1, 1), (Z, 2, 1))
E_GROUPS = (((X, 0, 2), (Y, 2, 1), (Z, 3, 1)), ((Z, 0, 2), (Y, 2, 1), (X, 3, 1)))

SHAPES = dict(
    series=((ROWS, LOOKBACK), BF16),
    w_embed=((LOOKBACK, WIDTH), BF16),
    w_query=((WIDTH, WIDTH), BF16),
    w_key=((WIDTH, WIDTH), BF16),
    w_value=((WIDTH, WIDTH), BF16),
    w_out=((WIDTH, WIDTH), BF16),
    proj=((KP, ROWS), BF16),
    cot=((ROWS, WIDTH), BF16),
    series_t=((LOOKBACK, ROWS), BF16),
    hid=((ROWS, WIDTH), BF16),
    hid_t=((WIDTH, ROWS), BF16),
    key_n=((PAIRS, KP, 128), F32),
    key_r=((PAIRS, KP, 128), F32),
    key_in=((PAIRS, 128, 512), BF16),
    key_out=((PAIRS, 512, 128), BF16),
    val_in=((PAIRS, 256, 512), BF16),
    val_out=((PAIRS, 512, 128), BF16),
    proj_t=((ROWS, KP), BF16),
    w_out_t=((WIDTH, WIDTH), BF16),
    w_query_t=((WIDTH, WIDTH), BF16),
    ph_core=((512, 128), F32),
    ph_plane=((15, 32, 128), F32),
    ph_x=((4, 32, 128), F32),
    ph=((1024, 128), F32),
)
LOADS = ("w_embed", "proj", "w_query", "cot", "w_out", "w_key", "w_value")
N_COPIES = 5 + 3 * 7 + 2 * 3 * 7


def layer_kernel(*refs):
    names = ("series", "w_embed", "w_query", "w_key", "w_value", "w_out", "proj", "cot")
    hbm = dict(zip(names, refs[:8]))
    out_hbm, embed_hbm, attn_hbm = refs[8:11]
    refs = refs[11:]
    v = dict(zip(SHAPES, refs[: len(SHAPES)]))
    for slot, name in enumerate(("att", "g_query", "g_hid", "out")):
        v[name] = v["series"].at[:, pl.ds(slot * WIDTH, WIDTH)]
    for slot, name in enumerate(("q_n", "g_att")):
        v[name] = v["w_embed"].at[pl.ds(slot * ROWS, ROWS)]
    refs = refs[len(SHAPES) :]
    s_bufs, q0_bufs, q1_bufs, e1_bufs = (refs[6 * i : 6 * i + 6] for i in range(4))
    e0_bufs = refs[24:29] + (s_bufs[0],)
    send, recv, load_sem, store_sem = refs[29:]
    v["q_r"] = e1_bufs[0]
    v["ph_in"] = e0_bufs[0].at[0]
    v["ph_half"] = e0_bufs[0].at[1, pl.ds(0, 512)]
    for side in range(2):
        where = pl.ds(side * KP, KP)
        v["gk", side] = v["hid_t"].at[where, pl.ds(0, WIDTH)]
        v["gv", side] = v["hid_t"].at[where, pl.ds(WIDTH, WIDTH)]
        v["back", side] = v["g_query"].at[where]
        v["ph_t", side] = v["g_hid"].at[pl.ds(0, WIDTH), pl.ds(side * KP, KP)]
    here = position()
    core, plane = here["c"], here["y"] * 4 + here["z"]
    base = core * 512

    def plane_device(step):
        there = lax.rem(plane + step, 16)
        return (here["x"] * 8 + lax.div(there, 4) * 2 + core, lax.rem(there, 4))

    loads = {}
    for slot, name in enumerate(LOADS):
        loads[name] = pltpu.make_async_copy(hbm[name], v[name], load_sem.at[slot])
    series_loads = []
    for block in range(LOADS_OF_SERIES):
        where = pl.ds(block * 256, 256)
        series_loads.append(
            pltpu.make_async_copy(
                hbm["series"].at[where], v["series"].at[where], load_sem.at[len(LOADS) + block]
            )
        )
    loads["w_embed"].start()
    for made in series_loads:
        made.start()
    loads["proj"].start()

    barrier = pltpu.get_barrier_semaphore()
    others = [moved(here, c=1)]
    others += [moved(here, x=step) for step in (1, 2, 3)]
    others += [plane_device(step) for step in range(1, 16)]
    for device in others:
        pl.semaphore_signal(barrier, inc=1, device_id=device, device_id_type=MESH)

    pool = Pool(send, recv)
    sum_s = Sum(here, pool, S_GROUPS, s_bufs, True)
    sum_q = [Sum(here, pool, Q_GROUPS, bufs, True) for bufs in (q0_bufs, q1_bufs)]
    sum_e = [Sum(here, pool, E_GROUPS[i], bufs) for i, bufs in enumerate((e0_bufs, e1_bufs))]

    lane = lax.broadcasted_iota(jnp.int32, (256, 128), 1) & 64
    row = lax.broadcasted_iota(jnp.int32, (256, 128), 0) & 64
    ones = jnp.where(lane == row, 1.0 / 64, 0.0).astype(BF16)

    def head_mean(values):
        return dot(jnp.concatenate(hi_lo(values), 1), ones)

    loads["w_embed"].wait()
    for block in range(BLOCKS):
        series_loads[2 * block].wait()
        series_loads[2 * block + 1].wait()
        if block == 1:
            for name in LOADS[2:]:
                loads[name].start()
        where = pl.ds(block * BLOCK, BLOCK)
        v["hid"][where] = dot(v["series"][where], v["w_embed"][...]).astype(BF16)
    loads["proj"].wait()
    part = dot(v["proj"][...], v["hid"][...])
    for pair in range(PAIRS):
        v["ph_in"][pl.ds(pair * 256, 256)] = part[:, pair * 128 : pair * 128 + 128]

    pl.semaphore_wait(barrier, len(others))
    across = pool.batch(v["ph_core"])
    across.add(v["ph_in"].at[rows((1 - core) * 512, 512)], v["ph_core"], moved(here, c=1))

    across.wait_recv()
    v["ph_half"][...] = v["ph_in"][rows(base, 512)] + v["ph_core"][...]
    scattered = pool.batch(v["ph_plane"])
    for step in range(1, 16):
        there = lax.rem(plane + step, 16)
        scattered.add(
            v["ph_half"].at[rows(there * 32, 32)], v["ph_plane"].at[step - 1], plane_device(step)
        )

    @pl.loop(0, 8)
    def _(part):
        where = rows(part * 256, 256)
        v["series_t"][where] = v["series"][:, where].T

    loads["w_query"].wait()

    @pl.loop(0, BLOCKS)
    def _(block):
        where = rows(block * BLOCK, BLOCK)
        query = dot(v["hid"][where], v["w_query"][...])
        for pair in range(PAIRS):
            part = query[:, pair * 128 : pair * 128 + 128]
            factor = lax.rsqrt(head_mean(part * part) + 1e-06)
            v["q_r"][pair, where] = factor
            v["q_n"][where, pl.ds(pair * 128, 128)] = (part * factor).astype(BF16)

    own = pl.multiple_of(plane * 32, 32)
    v["proj_t"][...] = v["proj"][...].T
    @pl.loop(0, 4)
    def _(part):
        got = dot(v["series_t"][rows(part * 512, 512)], v["proj_t"][...])
        unit = lax.div(part, 2) * 2
        where = rows(lax.rem(part, 2) * 512, 512)
        sum_s.data[unit, where] = got[:, :128]
        sum_s.data[unit + 1, where] = got[:, 128:]

    scattered.wait_recv()
    total = v["ph_half"][pl.ds(own, 32)]
    for step in range(15):
        total = total + v["ph_plane"][step]
    v["ph_x"][here["x"]] = total
    mine = v["ph_x"].at[here["x"]]
    shares = pool.batch(v["ph_x"].at[pl.ds(0, 3)])
    for step in (2, 1, 3):
        shares.add(mine, mine, moved(here, x=step))
    for group in range(3):
        sum_s.core(group)

    loads["cot"].wait()
    loads["w_out"].wait()
    v["w_out_t"][...] = v["w_out"][...].T
    v["w_query_t"][...] = v["w_query"][...].T

    @pl.loop(0, BLOCKS)
    def _(block):
        where = rows(block * BLOCK, BLOCK)
        grad = dot(v["cot"][where], v["w_out_t"][...]).astype(BF16)
        v["g_att"][where] = grad

    shares.wait_recv()
    whole = (v["ph_x"][0] + v["ph_x"][1]) + (v["ph_x"][2] + v["ph_x"][3])
    mine = v["ph"].at[rows(base + own, 32)]
    mine[...] = whole
    spread = pool.batch(v["ph"].at[pl.ds(0, 480)])
    for step in range(1, 16):
        spread.add(mine, mine, plane_device(step))
    sum_s.step1()
    v["hid_t"][...] = v["hid"][...].T

    spread.wait_recv()
    mine = v["ph"].at[rows(base, 512)]
    passed = pool.batch(mine)
    passed.add(mine, mine, moved(here, c=1))
    passed.wait_recv()
    pool.drain([across, scattered])

    loads["w_key"].wait()
    loads["w_value"].wait()
    ph = jnp.concatenate([v["ph"][pl.ds(pair * 256, 256)] for pair in range(PAIRS)], 1)
    ph_hi, ph_lo = hi_lo(ph)
    low_half = lax.broadcasted_iota(jnp.int32, (256, 128), 1) < 64
    none = jnp.zeros((256, 128), BF16)
    keys = dot(ph_hi, v["w_key"][...]) + dot(ph_lo, v["w_key"][...])
    values = dot(ph_hi, v["w_value"][...]) + dot(ph_lo, v["w_value"][...])
    blank = jnp.zeros((64, 256), BF16)
    for pair in range(PAIRS):
        part = keys[:, pair * 128 : pair * 128 + 128]
        factor = lax.rsqrt(head_mean(part * part) + 1e-06)
        normed = part * factor
        v["key_n"][pair] = normed
        v["key_r"][pair] = factor
        eighth = (normed * 0.125).astype(BF16)
        v["key_out"][pair, :256] = jnp.where(low_half, eighth, none)
        v["key_out"][pair, 256:] = jnp.where(low_half, none, eighth)
        turned = eighth.T
        v["key_in"][pair, :64, :256] = turned[:64]
        v["key_in"][pair, 64:, 256:] = turned[64:]
        v["key_in"][pair, :64, 256:] = blank
        v["key_in"][pair, 64:, :256] = blank
        val_hi, val_lo = hi_lo(values[:, pair * 128 : pair * 128 + 128])
        v["val_out"][pair, :256] = jnp.where(low_half, val_hi, none)
        v["val_out"][pair, 256:] = jnp.where(low_half, none, val_hi)
        for index, value in enumerate((val_hi, val_lo)):
            turned = value.T
            at = index * 128
            v["val_in"][pair, at : at + 64, :256] = turned[:64]
            v["val_in"][pair, at + 64 : at + 128, 256:] = turned[64:]
            v["val_in"][pair, at : at + 64, 256:] = blank
            v["val_in"][pair, at + 64 : at + 128, :256] = blank

    def attention(pair):
        sums = sum_q[pair // 2].data
        first = (pair % 2) * 128
        lanes_of = pl.ds(pair * 128, 128)
        for part in range(4):
            sums[0, pl.ds(part * 256 + first, 128)] = jnp.zeros((128, 128), F32)

        @pl.loop(0, ROWS // ATTENTION_BLOCK, unroll=2)
        def _(block):
            where = rows(block * ATTENTION_BLOCK, ATTENTION_BLOCK)
            query = v["q_n"][where, lanes_of]
            grad = v["g_att"][where, lanes_of]
            scores = dot(query, v["key_in"][pair])
            grad_probs = dot(jnp.concatenate([grad, grad], 1), v["val_in"][pair])
            query_t, grad_t = query.T, grad.T
            probs_b, grad_scores = [], []
            for head in range(2):
                lanes = slice(head * 256, head * 256 + 256)
                expo = jnp.exp(scores[:, lanes])
                probs = expo * (1.0 / jnp.sum(expo, axis=1, keepdims=True))
                grad_p = grad_probs[:, lanes]
                inner = jnp.sum(probs * grad_p, axis=1, keepdims=True)
                probs_b.append(probs.astype(BF16))
                grad_scores.append((probs * (grad_p - inner)).astype(BF16))
                for at, got in (
                    (0, dot(query_t[head * 64 : head * 64 + 64], grad_scores[head])),
                    (512, dot(grad_t[head * 64 : head * 64 + 64], probs_b[head])),
                ):
                    for side in range(2):
                        rest = pl.ds(at + side * 256 + first + head * 64, 64)
                        sums[0, rest] = sums[0, rest] + got[:, side * 128 : side * 128 + 128]
            attended = dot(jnp.concatenate(probs_b, 1), v["val_out"][pair])
            v["att"][where, lanes_of] = attended.astype(BF16)
            grad_n = dot(jnp.concatenate(grad_scores, 1), v["key_out"][pair])
            normed = query.astype(F32)
            grad_q = v["q_r"][pair, where] * (grad_n - normed * head_mean(grad_n * normed))
            v["g_query"][where, lanes_of] = grad_q.astype(BF16)

    def weight_grads(quad):
        both = pl.ds(quad * 256, 256)
        sums = sum_q[quad].data
        got = dot(v["att"][:, both].T, v["cot"][...])
        for part in range(4):
            sums[2, pl.ds(part * 256, 256)] = got[:, part * 128 : part * 128 + 128]
        sum_q[quad].core(0)
        got = dot(v["hid_t"][...], v["g_query"][:, both])
        for part in range(2):
            sums[1, pl.ds(part * 512, 512)] = got[:, part * 128 : part * 128 + 128]
        sum_q[quad].core(1)
        sum_q[quad].core(2)

    attention(0)
    sum_s.step2()
    attention(1)
    weight_grads(0)
    sum_s.step3()
    attention(2)
    attention(3)
    sum_q[0].step1()
    sum_s.step4()

    @pl.loop(0, BLOCKS)
    def _(block):
        where = rows(block * BLOCK, BLOCK)
        v["g_hid"][where] = (
            v["cot"][where].astype(F32) + dot(v["g_query"][where], v["w_query_t"][...])
        ).astype(BF16)

    weight_grads(1)

    def embed_part(index):
        @pl.loop(0, 2)
        def _(part):
            got = dot(v["series_t"][rows(index * 1024 + part * 512, 512)], v["g_hid"][...])
            where = rows(part * 512, 512)
            for unit in range(4):
                sum_e[index].data[unit, where] = got[:, unit * 128 : unit * 128 + 128]

        for group in range(3):
            sum_e[index].core(group)

    sum_s.settle()
    embed_part(0)
    sum_q[1].step1()
    sum_q[0].step2()
    embed_part(1)
    sum_e[0].step1()
    sum_s.step5()
    sum_e[1].step1()
    sum_q[1].step2()
    sum_q[0].step3()

    @pl.loop(0, BLOCKS)
    def _(block):
        where = rows(block * BLOCK, BLOCK)
        v["out"][where] = (
            v["hid"][where].astype(F32) + dot(v["att"][where], v["w_out"][...])
        ).astype(BF16)

    stores = []

    def store(src, dst):
        made = pltpu.make_async_copy(src, dst, store_sem.at[len(stores)])
        made.start()
        stores.append(made)

    store(v["out"], out_hbm)
    sum_e[0].step2()
    sum_q[1].step3()
    sum_q[0].step4()
    sum_e[1].step2()
    sum_e[0].step3()
    sum_q[1].step4()
    sum_s.step6()
    sum_q[0].step5()
    sum_e[1].step3()
    sum_e[0].step4()
    sum_q[1].step5()
    sum_e[1].step4()
    sum_e[0].step5()
    sum_q[0].step6()
    sum_s.all7()
    sum_q[0].all7()
    for side, part in enumerate(hi_lo(ph)):
        v["ph_t", side][...] = part.T
    sum_q[1].step6()
    sum_e[1].step5()
    sum_q[1].all7()
    for one in sum_e:
        one.settle()
    for one in sum_q:
        one.finish()

    for quad in range(2):
        for half in range(2):
            pair = quad * 2 + half
            lanes = pl.ds(pair * 128, 128)
            turned = []
            for at in (0, 512):
                turned.append(
                    jnp.concatenate(
                        [
                            sum_q[quad].out[0, pl.ds(at + side * 256 + half * 128, 128)]
                            for side in range(2)
                        ],
                        1,
                    ).T
                )
            grad_n = turned[0] * 0.125
            normed = v["key_n"][pair]
            grad_k = v["key_r"][pair] * (grad_n - normed * head_mean(grad_n * normed))
            for index, (name, value) in enumerate((("gk", grad_k), ("gv", turned[1]))):
                for side, part in enumerate(hi_lo(value)):
                    v[name, side][:, lanes] = part
    back = dot_t(v["gk", 0][...], v["w_key"][...]) + dot_t(v["gk", 1][...], v["w_key"][...])
    back = back + dot_t(v["gv", 0][...], v["w_value"][...]) + dot_t(v["gv", 1][...], v["w_value"][...])
    for side, part in enumerate(hi_lo(back)):
        v["back", side][...] = part
    for index, name in enumerate(("gk", "gv")):
        got = dot(v["ph_t", 0][...], v[name, 0][...]) + dot(v["ph_t", 0][...], v[name, 1][...])
        got = (got + dot(v["ph_t", 1][...], v[name, 0][...])) * NORM
        for part in range(4):
            where = (part // 2, pl.ds((part % 2) * 512, 512))
            sum_q[index].data[where] = got[:, part * 128 : part * 128 + 128]
            store(sum_q[index].data.at[where], attn_hbm.at[1 + index, :, pl.ds(part * 128, 128)])
    for quad in range(2):
        out = sum_q[quad].out

        @pl.loop(1, 3)
        def _(unit):
            out[unit] = out[unit] * NORM

        for part in range(2):
            store(
                out.at[1, pl.ds(part * 512, 512)],
                attn_hbm.at[0, :, pl.ds(quad * 256 + part * 128, 128)],
            )
        for part in range(4):
            store(
                out.at[2, pl.ds(part * 256, 256)],
                attn_hbm.at[3, pl.ds(quad * 256, 256), pl.ds(part * 128, 128)],
            )
    sum_e[0].step6()
    sum_e[1].step6()
    for index in range(2):

        @pl.loop(0, 4)
        def _(part):
            where = rows(part * 256, 256)
            left = jnp.concatenate([sum_s.out[index * 2 + side, where] for side in range(2)], 1)
            left_hi, left_lo = hi_lo(left)
            got = dot(left_hi, v["back", 0][...]) + dot(left_hi, v["back", 1][...])
            got = got + dot(left_lo, v["back", 0][...])
            for unit in range(4):
                sum_e[index].data[unit, where] = got[:, unit * 128 : unit * 128 + 128]

    for index in range(2):
        for group, (_, start, size) in enumerate(E_GROUPS[index]):
            sum_e[index].step7(group)
        sum_e[index].finish()
        for unit in range(4):

            @pl.loop(0, 4)
            def _(part):
                where = (unit, rows(part * 256, 256))
                sum_e[index].out[where] = (
                    sum_e[index].out[where] + sum_e[index].data[where]
                ) * NORM

            store(
                sum_e[index].out.at[unit],
                embed_hbm.at[pl.ds(index * 1024, 1024), pl.ds(unit * 128, 128)],
            )
    pool.drain()
    for made in stores:
        made.wait()


def local(series, w_embed, w_query, w_key, w_value, w_out, proj, cotangent):
    anywhere = pl.BlockSpec(memory_space=pl.ANY)
    return pl.pallas_call(
        layer_kernel,
        out_shape=(
            jax.ShapeDtypeStruct((ROWS, WIDTH), BF16),
            jax.ShapeDtypeStruct((LOOKBACK, WIDTH), F32),
            jax.ShapeDtypeStruct((4, WIDTH, WIDTH), F32),
        ),
        in_specs=[anywhere] * 8,
        out_specs=(anywhere,) * 3,
        scratch_shapes=[VMEM(shape, dtype) for shape, dtype in SHAPES.values()]
        + sum_bufs(4)
        + sum_bufs(3) * 2
        + sum_bufs(4)
        + sum_bufs(4, False)
        + [
            pltpu.SemaphoreType.DMA((N_COPIES,)),
            pltpu.SemaphoreType.DMA((N_COPIES,)),
            pltpu.SemaphoreType.DMA((len(LOADS) + LOADS_OF_SERIES,)),
            pltpu.SemaphoreType.DMA((32,)),
        ],
        compiler_params=pltpu.CompilerParams(
            collective_id=0, has_side_effects=True, vmem_limit_bytes=63 * 1024 * 1024
        ),
    )(series, w_embed, w_query, w_key, w_value, w_out, proj, cotangent)


def solution(mesh):
    return jax.shard_map(
        local,
        mesh=mesh,
        in_specs=(
            P(("var", "grp"), None),
            P(),
            P(),
            P(),
            P(),
            P(),
            P(None, ("var", "grp")),
            P(("var", "grp"), None),
        ),
        out_specs=(P(("var", "grp"), None), P(), P()),
        check_vma=False,
    )
```
